32 devices in a mesh: freq: 2 (over x), strip: 16 (over z, y, core).
Axes of the slice: x: 2, y: 2, z: 4, core: 2. Of those that a mesh axis runs over, the one named last changes fastest.
Arguments:
- source_field: float32 [2, 4, 1024, 1024], P(None, 'freq', 'strip'), may hold values from -6 to 6
- receiver_field: float32 [2, 4, 1024, 1024], P(None, 'freq', 'strip'), may hold values from -6 to 6
- velocity: float32 [2, 1024, 1024], P('freq', 'strip'), may hold values from 0.625 to 1.6
- slice_owner: int32 [2], replicated, may hold values from 0 to 1, each once
Outputs:
- depth_image: float32 [2, 1024, 1024], P(None, 'strip', 'freq')
- source_out: float32 [2, 4, 1024, 1024], P(None, 'freq', 'strip')
- receiver_out: float32 [2, 4, 1024, 1024], P(None, 'freq', 'strip')
The draws below stay inside these ranges and needn't reach their ends.
Inputs may be any that keep to these rules, and one draw needn't show every extreme that they name: A permutation of the 2 velocity slices; depth step d reads slice slice_owner[d], which index slice_owner[d] // 1 of freq holds.
All inputs are finite; a program needn't handle non-finite values.
Results may differ from the reference program's by a relative error of at most 0.00011.
Values sent between devices are 32-bit elements; how exact they have to be, the bound alone decides.
No kernel may reach another device: no remote copies, remote signals or barrier semaphores. Data moves between devices by JAX's collectives and lax.ppermute only.
A program may use at most 128 MiB of HBM per device.

```python
import math
import jax
import jax.numpy as jnp
from jax import lax

NX = 1024
NY = 1024
DEPTHS = 2
NFREQ = 4
VSLICES = 2


def block_scale(rng, dims, pieces, least, top_value):
    gain = 1.0
    for dim, blocks in pieces:
        heights = jax.random.uniform(jax.random.fold_in(jax.random.fold_in(rng, 6), dim), (blocks,), jnp.float32, least / len(pieces), top_value / len(pieces))
        gain = gain * jnp.repeat(jnp.exp(heights), dims[dim] // blocks).reshape((-1,) + (1,) * (len(dims) - 1 - dim))
    return gain


def noise(own_key, extent, spread, bound, split=(), kind=jnp.bfloat16):
    gain = block_scale(own_key, extent, split, -0.22, 0.18) if split else 1.0
    array = jax.random.normal(own_key, extent, jnp.float32) * spread * gain
    return jnp.minimum(jnp.maximum(array, -bound), bound).astype(kind)


def setup_inputs(seed: int = 0) -> dict:
    seeds = jax.random.split(jax.random.key(seed), 5)
    source_field = noise(seeds[0], (2, NFREQ, NX, NY), 1.0, 6.0, ((1, 2), (2, 16)), jnp.float32)
    receiver_field = noise(seeds[1], (2, NFREQ, NX, NY), 1.0, 6.0, ((1, 2), (2, 16)), jnp.float32)
    velocity = jnp.clip(jnp.exp(math.log(1.6) - 0.94000727 * jax.random.uniform(seeds[2], (VSLICES, NX, NY), jnp.float32) ** block_scale(seeds[2], (VSLICES, NX, NY), ((0, 2), (1, 16)), -0.2, 0.2)), 0.625, 1.6)
    slice_owner = jax.random.permutation(seeds[3], VSLICES).astype(jnp.int32)
    return {"source_field": source_field, "receiver_field": receiver_field, "velocity": velocity, "slice_owner": slice_owner}


step_length = 0.15
omega_top = 1.2
stencil_gain = 0.05
stencil_damping = 0.1

def centered(length):
    position = jnp.arange(length, dtype=jnp.int32)
    shifted = jnp.where(position < length // 2, position, position - length)
    return shifted.astype(jnp.float32) * (2.0 * math.pi / length)

def laplace(field):
    padded = jnp.pad(field, ((0, 0), (1, 1), (1, 1)))
    return padded[:, 2:, 1:-1] + padded[:, :-2, 1:-1] + padded[:, 1:-1, 2:] + padded[:, 1:-1, :-2] - 4.0 * field

def reference(source_field, receiver_field, velocity, slice_owner):
    wave_x = centered(NX)
    wave_y = centered(NY)
    angular = (omega_top * (jnp.arange(NFREQ, dtype=jnp.int32) + 1).astype(jnp.float32) / NFREQ)[:, None, None]
    argument = angular * angular - (wave_x[:, None] * wave_x[:, None] + wave_y[None, :] * wave_y[None, :])[None]
    radius = jnp.sqrt(jnp.abs(argument))
    travel = argument >= 0.0
    trans_real = jnp.where(travel, jnp.cos(step_length * radius), jnp.exp(-step_length * radius))
    trans_imag = jnp.where(travel, jnp.sin(step_length * radius), jnp.zeros_like(radius))
    fields = [lax.complex(source_field[0], source_field[1]), lax.complex(receiver_field[0], receiver_field[1])]
    field_signs = [-1.0, 1.0]
    images = []
    for depth_step in range(DEPTHS):
        speed = lax.dynamic_index_in_dim(velocity, slice_owner[depth_step], 0, keepdims=False)
        gap = 1.0 / speed - 1.0
        weight = stencil_gain * (speed * speed - 1.0)[None] * angular / omega_top
        updated = []
        for which in range(2):
            sign_value = field_signs[which]
            transfer = lax.complex(trans_real, sign_value * trans_imag)
            field = jnp.fft.ifft2(jnp.fft.fft2(fields[which], axes=(1, 2)) * transfer, axes=(1, 2))
            phase = sign_value * angular * step_length * gap[None]
            field = field * lax.complex(jnp.cos(phase), jnp.sin(phase))
            coefficient = lax.complex(stencil_damping * weight, sign_value * weight)
            field = field + coefficient * laplace(field)
            updated.append(field)
        fields = updated
        images.append(lax.optimization_barrier(jnp.sum(jnp.real(fields[0]) * jnp.real(fields[1]) + jnp.imag(fields[0]) * jnp.imag(fields[1]), axis=0)))
    depth_image = jnp.stack(images)
    source_out = jnp.stack([jnp.real(fields[0]), jnp.imag(fields[0])])
    receiver_out = jnp.stack([jnp.real(fields[1]), jnp.imag(fields[1])])
    return (depth_image, source_out, receiver_out)
```

```python
import functools
import math

import jax
import jax.numpy as jnp
import numpy as np
from jax import lax
from jax.experimental import pallas as pl
from jax.experimental.pallas import tpu as pltpu
from jax.sharding import PartitionSpec as P

DEPTHS = 2

step_length = 0.15
omega_top = 1.2
stencil_gain = 0.05
stencil_damping = 0.1

LANES = 128
ROWS = 16
VMEM_LIMIT = 56 * 1024 * 1024
F32 = jnp.float32
BF16 = jnp.bfloat16


def halves(table):
    table = np.asarray(table, np.float32)
    high = table.astype(jnp.bfloat16)
    low = (table - high.astype(np.float32)).astype(jnp.bfloat16)
    return high, low


def point_tables():
    index = np.arange(LANES)
    angle = 2.0 * np.pi * (index[:, None] * index[None, :] % LANES) / LANES
    cosine, sine = np.cos(angle), np.sin(angle)
    forward = np.block([[cosine, -sine], [sine, cosine]])
    return forward, forward.T


def twiddles(radix):
    length = radix * LANES
    angle = 2.0 * np.pi * (np.arange(radix)[:, None] * np.arange(LANES)[None, :]) / length
    return np.stack([np.cos(angle), -np.sin(angle)]).astype(np.float32)


def small_dft(real, imag, sign):
    count = len(real)
    if count == 1:
        return list(real), list(imag)
    even = small_dft(real[0::2], imag[0::2], sign)
    odd = small_dft(real[1::2], imag[1::2], sign)
    half = count // 2
    top_real, top_imag, low_real, low_imag = [], [], [], []
    for k in range(half):
        o_re, o_im = odd[0][k], odd[1][k]
        if k == 0:
            t_re, t_im = o_re, o_im
        elif 4 * k == count:
            t_re, t_im = (-o_im, o_re) if sign > 0 else (o_im, -o_re)
        elif 8 * k == count:
            h = math.sqrt(0.5)
            t_re, t_im = ((o_re - o_im) * h, (o_im + o_re) * h) if sign > 0 else ((o_re + o_im) * h, (o_im - o_re) * h)
        elif 8 * k == 3 * count:
            h = math.sqrt(0.5)
            t_re, t_im = ((-o_re - o_im) * h, (o_re - o_im) * h) if sign > 0 else ((o_im - o_re) * h, (-o_re - o_im) * h)
        else:
            w_re, w_im = math.cos(2 * math.pi * k / count), sign * math.sin(2 * math.pi * k / count)
            t_re, t_im = o_re * w_re - o_im * w_im, o_re * w_im + o_im * w_re
        top_real.append(even[0][k] + t_re)
        top_imag.append(even[1][k] + t_im)
        low_real.append(even[0][k] - t_re)
        low_imag.append(even[1][k] - t_im)
    return top_real + low_real, top_imag + low_imag


def parts(value):
    high = value.astype(BF16)
    return high, (value - high.astype(F32)).astype(BF16)


def dot(left, right):
    return jnp.dot(left, right, preferred_element_type=F32)


def dot_right(high, low, table):
    return dot(high, table[0]) + dot(low, table[0]) + dot(high, table[1])


def dot_left(both, data_high, data_low):
    size = both.shape[0] // 2
    first = dot(both[...], data_high)
    return first[:size] + first[size:] + dot(both[:size], data_low)


def lanes(k, count=1):
    return slice(k * LANES, (k + count) * LANES)


def forward_into(load, row, twist, high, low, index):
    radix = twist.shape[1]
    real, imag = zip(*[load(a) for a in range(radix)])
    real, imag = small_dft(list(real), list(imag), -1)
    for k in range(radix):
        re, im = real[k], imag[k]
        if k:
            c, s = twist[0, k : k + 1, :], twist[1, k : k + 1, :]
            re, im = re * c - im * s, re * s + im * c
        for part, value in ((0, re), (1, im)):
            h, l = parts(value)
            high[index(k) + (row, lanes(part))] = h
            low[index(k) + (row, lanes(part))] = l


def wait_all(copies):
    for copy in copies:
        copy.start()
    for copy in copies:
        copy.wait()


def copier(sems):
    made = []

    def add(source, target):
        made.append(pltpu.make_async_copy(source, target, sems.at[len(made)]))

    return made, add


def first_kernel(ids, source, receiver, table, twist, keep, send, high, low):
    z, core = ids[0], ids[2]
    groups, half = keep.shape[0], keep.shape[1]
    rows = source.shape[2]
    for e in range(groups):
        field = z ^ e
        which, number = lax.rem(field, 2), lax.div(field, 2)

        def chunk(t, carry, e=e, which=which, number=number):
            row = pl.ds(pl.multiple_of(t * ROWS, ROWS), ROWS)

            def load(a):
                return tuple(
                    jnp.where(which == 0, source[part, number, row, lanes(a)], receiver[part, number, row, lanes(a)])
                    for part in (0, 1)
                )

            forward_into(load, row, twist, high, low, lambda k: (e, k))
            return carry

        lax.fori_loop(0, rows // ROWS, chunk, 0)
        for out, start in ((keep, core * half), (send, (1 - core) * half)):
            h = high[e, pl.ds(start, half)].reshape(half * rows, 2 * LANES)
            l = low[e, pl.ds(start, half)].reshape(half * rows, 2 * LANES)
            result = dot_right(h, l, table)
            for part in (0, 1):
                out[e, :, part] = result[:, lanes(part)].reshape(half, rows, LANES)


def first_transform(ids, source, receiver, groups, tab):
    rows, width = source.shape[2:]
    radix = width // LANES
    out = jax.ShapeDtypeStruct((groups, radix // 2, 2, rows, LANES), F32)
    scratch = pltpu.VMEM((groups, radix, rows, 2 * LANES), BF16)
    return pl.pallas_call(
        first_kernel,
        out_shape=(out, out),
        in_specs=[pl.BlockSpec(memory_space=pltpu.SMEM)] + [pl.BlockSpec(memory_space=pltpu.VMEM)] * 4,
        out_specs=(pl.BlockSpec(memory_space=pltpu.VMEM),) * 2,
        scratch_shapes=[scratch, scratch],
        compiler_params=pltpu.CompilerParams(vmem_limit_bytes=VMEM_LIMIT),
        name="first_transform",
    )(ids, source, receiver, tab["right_forward"], tab["twist_y"])


def shift_columns(data, filt_re, filt_im, ahead, back, twist, high, low, line):
    blocks = data.shape[0]
    radix = twist.shape[1]
    for pair in range(0, blocks, 2):

        def fold(t, carry, pair=pair):
            off = pl.multiple_of(t * ROWS, ROWS)
            for kk in (0, 1):
                real = [data[pair + kk, 0, pl.ds(a * LANES + off, ROWS), :] for a in range(radix)]
                imag = [data[pair + kk, 1, pl.ds(a * LANES + off, ROWS), :] for a in range(radix)]
                real, imag = small_dft(real, imag, -1)
                for k in range(radix):
                    re, im = real[k], imag[k]
                    if k:
                        c, s = twist[0, k, pl.ds(off, ROWS), :], twist[1, k, pl.ds(off, ROWS), :]
                        re, im = re * c - im * s, re * s + im * c
                    for part, value in ((0, re), (1, im)):
                        h, l = parts(value)
                        high[k, pl.ds(part * LANES + off, ROWS), lanes(kk)] = h
                        low[k, pl.ds(part * LANES + off, ROWS), lanes(kk)] = l
            return carry

        lax.fori_loop(0, LANES // ROWS, fold, 0)

        def spectral(k, carry, pair=pair):
            value = dot_left(ahead, high[k], low[k])
            re, im = value[:LANES], value[LANES:]
            fr = jnp.concatenate([filt_re[pair, k], filt_re[pair + 1, k]], axis=1)
            fi = jnp.concatenate([filt_im[pair, k], filt_im[pair + 1, k]], axis=1)
            both = jnp.concatenate([re * fr - im * fi, re * fi + im * fr], axis=0)
            h, l = parts(both)
            line[k] = dot_left(back, h, l)
            return carry

        lax.fori_loop(0, radix, spectral, 0, unroll=4)

        def unfold(t, carry, pair=pair):
            off = pl.multiple_of(t * ROWS, ROWS)
            for kk in (0, 1):
                real, imag = [], []
                for k in range(radix):
                    re = line[k, pl.ds(off, ROWS), lanes(kk)]
                    im = line[k, pl.ds(LANES + off, ROWS), lanes(kk)]
                    if k:
                        c, s = twist[0, k, pl.ds(off, ROWS), :], twist[1, k, pl.ds(off, ROWS), :]
                        re, im = re * c + im * s, im * c - re * s
                    real.append(re)
                    imag.append(im)
                real, imag = small_dft(real, imag, 1)
                for a in range(radix):
                    data[pair + kk, 0, pl.ds(a * LANES + off, ROWS), :] = real[a]
                    data[pair + kk, 1, pl.ds(a * LANES + off, ROWS), :] = imag[a]
            return carry

        lax.fori_loop(0, LANES // ROWS, unfold, 0)


def enter_kernel(groups, across, rows, ids, filt_re, filt_im, ahead, back, twist, *refs):
    pieces = refs[: groups * across]
    keep, send, data, high, low, line, edge, sems = refs[groups * across :]
    z, y, core = ids[0], ids[1], ids[2]
    count = groups * across
    copies, add = copier(sems)
    for e in range(groups):
        for r in range(across):
            block = (z ^ e) * across + (y ^ r)
            for h in (0, 1):
                start = pl.multiple_of((2 * block + (core ^ h)) * rows, rows)
                add(pieces[e * across + r].at[h], data.at[:, :, pl.ds(start, rows), :])
    wait_all(copies)
    shift_columns(data, filt_re, filt_im, ahead, back, twist, high, low, line)
    total = data.shape[2]
    for i in range(count):
        for h in (0, 1):
            start = (2 * i + h) * rows
            for side, row in ((0, start - 1), (1, start + rows)):
                if 0 <= row < total:
                    edge[h, :, :, 2 * i + side : 2 * i + side + 1, :] = data[:, :, row : row + 1, :]
                else:
                    edge[h, :, :, 2 * i + side : 2 * i + side + 1, :] = jnp.zeros(data.shape[:2] + (1, LANES), F32)
    copies, add = copier(sems)
    for out, parity in ((keep, core), (send, 1 - core)):
        for i in range(count):
            start = pl.multiple_of((2 * i + parity) * rows, rows)
            add(data.at[:, :, pl.ds(start, rows), :], out.at[:, :, pl.ds(i * rows, rows), :])
        add(edge.at[parity], out.at[:, :, pl.ds(count * rows, 2 * count), :])
    wait_all(copies)


def leave_kernel(groups, across, rows, ids, filt_re, filt_im, ahead, back, twist, mine, other, *refs):
    outs = refs[: 2 * groups]
    data, high, low, line, edge, sems = refs[2 * groups :]
    z, y, core = ids[0], ids[1], ids[2]
    count = groups * across
    copies, add = copier(sems)
    for piece, parity in ((mine, core), (other, 1 - core)):
        for i in range(count):
            start = pl.multiple_of((2 * i + parity) * rows, rows)
            add(piece.at[:, :, pl.ds(i * rows, rows), :], data.at[:, :, pl.ds(start, rows), :])
    wait_all(copies)
    shift_columns(data, filt_re, filt_im, ahead, back, twist, high, low, line)
    blocks, _, total, _ = data.shape
    for b in range(2 * count):
        for side, row in ((0, b * rows - 1), (1, (b + 1) * rows)):
            for k in range(blocks):
                for part in (0, 1):
                    at = (2 * k + part) * 2 + side
                    if 0 <= row < total:
                        edge[b, at : at + 1, :] = data[k, part, row : row + 1, :]
                    else:
                        edge[b, at : at + 1, :] = jnp.zeros((1, LANES), F32)
    copies, add = copier(sems)
    for e in range(groups):
        for h in (0, 1):
            block = 2 * ((z ^ e) * across + y) + (core ^ h)
            start = pl.multiple_of(block * rows, rows)
            out = outs[2 * e + h]
            for k in range(blocks):
                for part in (0, 1):
                    add(data.at[k, part, pl.ds(start, rows), :], out.at[pl.ds((2 * k + part) * rows, rows), :])
            add(edge.at[block], out.at[pl.ds(2 * blocks * rows, 4 * blocks), :])
    wait_all(copies)


def column_scratch(half, total):
    radix = total // LANES
    return [
        pltpu.VMEM((half, 2, total, LANES), F32),
        pltpu.VMEM((radix, 2 * LANES, 2 * LANES), BF16),
        pltpu.VMEM((radix, 2 * LANES, 2 * LANES), BF16),
        pltpu.VMEM((radix, 2 * LANES, 2 * LANES), F32),
    ]


def column_specs():
    return [pl.BlockSpec(memory_space=pltpu.SMEM)] + [pl.BlockSpec(memory_space=pltpu.VMEM)] * 5


def enter_columns(ids, pieces, filt, tab, groups, across):
    _, half, _, rows, _ = pieces[0].shape
    count = groups * across
    total = 2 * count * rows
    out = jax.ShapeDtypeStruct((half, 2, count * rows + 2 * count, LANES), F32)
    return pl.pallas_call(
        functools.partial(enter_kernel, groups, across, rows),
        out_shape=(out, out),
        in_specs=column_specs() + [pl.BlockSpec(memory_space=pl.ANY)] * count,
        out_specs=(pl.BlockSpec(memory_space=pl.ANY),) * 2,
        scratch_shapes=column_scratch(half, total)
        + [pltpu.VMEM((2, half, 2, 2 * count, LANES), F32), pltpu.SemaphoreType.DMA((2 * count + 2,))],
        compiler_params=pltpu.CompilerParams(vmem_limit_bytes=VMEM_LIMIT),
        name="enter_columns",
    )(ids, *filt, tab["left_forward"], tab["left_inverse"], tab["twist_x"], *pieces)


def leave_columns(ids, mine, other, filt, tab, groups, across):
    half, _, own, _ = mine.shape
    count = groups * across
    rows = own // count
    total = 2 * own
    out = jax.ShapeDtypeStruct((2 * half * rows + 4 * half, LANES), F32)
    return pl.pallas_call(
        functools.partial(leave_kernel, groups, across, rows),
        out_shape=(out,) * (2 * groups),
        in_specs=column_specs() + [pl.BlockSpec(memory_space=pl.ANY)] * 2,
        out_specs=(pl.BlockSpec(memory_space=pl.ANY),) * (2 * groups),
        scratch_shapes=column_scratch(half, total)
        + [
            pltpu.VMEM((2 * count, 4 * half, LANES), F32),
            pltpu.SemaphoreType.DMA((max(2 * count, 2 * groups * (2 * half + 1)),)),
        ],
        compiler_params=pltpu.CompilerParams(vmem_limit_bytes=VMEM_LIMIT),
        name="leave_columns",
    )(ids, *filt, tab["left_forward"], tab["left_inverse"], tab["twist_x"], mine, other)


def inverse_rows(load, rows, table, twist, cosine, sine, store):
    radix = twist.shape[1]
    size = next(s for s in (48, 64, 80, 32, 16) if rows % s == 0)

    def chunk(t, carry):
        row = pl.ds(pl.multiple_of(t * size, ROWS), size)
        data = jnp.concatenate(
            [jnp.concatenate([load(k, 0, row), load(k, 1, row)], axis=1) for k in range(radix)], axis=0
        )
        result = dot_right(*parts(data), table)
        real, imag = [], []
        for k in range(radix):
            re = result[k * size : (k + 1) * size, lanes(0)]
            im = result[k * size : (k + 1) * size, lanes(1)]
            if k:
                c, s = twist[0, k : k + 1, :], twist[1, k : k + 1, :]
                re, im = re * c + im * s, im * c - re * s
            real.append(re)
            imag.append(im)
        real, imag = small_dft(real, imag, 1)
        for a in range(radix):
            c, s = cosine(row, lanes(a)), sine(row, lanes(a))
            store(0, row, lanes(a), real[a] * c - imag[a] * s)
            store(1, row, lanes(a), real[a] * s + imag[a] * c)
        return carry

    lax.fori_loop(0, rows // size, chunk, 0)


def laplace(center, above, below):
    rows, width = center.shape
    line = lax.broadcasted_iota(jnp.int32, center.shape, 0)
    place = lax.broadcasted_iota(jnp.int32, center.shape, 1)
    up = jnp.where(line == 0, above, pltpu.roll(center, 1, axis=0))
    down = jnp.where(line == rows - 1, below, pltpu.roll(center, rows - 1, axis=0))
    left = jnp.where(place == 0, 0.0, pltpu.roll(center, 1, axis=1))
    right = jnp.where(place == width - 1, 0.0, pltpu.roll(center, width - 1, axis=1))
    return (up + down) + (left + right) - 4.0 * center


def stencil(field, rows, halo, weight, sign):
    center = [field(part) for part in (0, 1)]
    bent = [laplace(center[part], halo(part, 0), halo(part, 1)) for part in (0, 1)]
    turn = weight * sign
    damp = weight * stencil_damping
    return (
        center[0] + damp * bent[0] - turn * bent[1],
        center[1] + damp * bent[1] + turn * bent[0],
    )


def middle_kernel(groups, across, rows, ids, back, ahead, twist, cosine, sine, weight, mine, other, keep, send, near, far, *scratch):
    data, field, fresh, high, low, sems = scratch
    z, y, core = ids[0], ids[1], ids[2]
    which = lax.rem(z, 2)
    sign = jnp.where(which == 0, -1.0, 1.0).astype(F32)
    half = mine.shape[0]
    count = groups * across
    own = count * rows
    copies, add = copier(sems)
    add(mine, data.at[pl.ds(core * half, half)])
    add(other, data.at[pl.ds((1 - core) * half, half)])
    wait_all(copies)

    def store(part, row, lane, value):
        field[part, row, lane] = value

    inverse_rows(
        lambda k, part, row: data[k, part, row, :],
        own + 2 * count,
        back,
        twist,
        lambda row, lane: cosine[row, lane],
        lambda row, lane: sine[row, lane],
        store,
    )

    def block(i, carry):
        row = pl.ds(pl.multiple_of(i * rows, rows), rows)
        new = stencil(
            lambda part: field[part, row, :],
            rows,
            lambda part, side: field[part, pl.ds(own + 2 * i + side, 1), :],
            weight[row, :],
            sign,
        )
        fresh[0, row, :] = new[0]
        fresh[1, row, :] = new[1]
        return carry

    lax.fori_loop(0, count, block, 0)

    copies, add = copier(sems)
    for out, parity in ((near, which), (far, 1 - which)):
        for t in range(groups // 2):
            start = pl.multiple_of(((parity + 2 * t) * across + y) * rows, rows)
            add(fresh.at[:, pl.ds(start, rows), :], out.at[:, t])
    for copy in copies:
        copy.start()

    def fold(t, carry):
        row = pl.ds(pl.multiple_of(t * ROWS, ROWS), ROWS)
        forward_into(lambda a: (fresh[0, row, lanes(a)], fresh[1, row, lanes(a)]), row, twist, high, low, lambda k: (k,))
        return carry

    lax.fori_loop(0, own // ROWS, fold, 0)
    for out, start in ((keep, core * half), (send, (1 - core) * half)):
        for k in range(half):
            result = dot_right(high[start + k], low[start + k], ahead)
            for part in (0, 1):
                out[k, part] = result[:, lanes(part)]
    for copy in copies:
        copy.wait()


def middle(ids, mine, other, factors, tab, groups, across):
    half, _, tall, _ = mine.shape
    count = groups * across
    own = tall - 2 * count
    rows = own // count
    radix = 2 * half
    width = radix * LANES
    out = jax.ShapeDtypeStruct((half, 2, own, LANES), F32)
    image = jax.ShapeDtypeStruct((2, groups // 2, rows, width), F32)
    vmem, hbm = pl.BlockSpec(memory_space=pltpu.VMEM), pl.BlockSpec(memory_space=pl.ANY)
    return pl.pallas_call(
        functools.partial(middle_kernel, groups, across, rows),
        out_shape=(out, out, image, image),
        in_specs=[pl.BlockSpec(memory_space=pltpu.SMEM)] + [vmem] * 6 + [hbm] * 2,
        out_specs=(vmem, vmem, hbm, hbm),
        scratch_shapes=[
            pltpu.VMEM((radix, 2, tall, LANES), F32),
            pltpu.VMEM((2, tall, width), F32),
            pltpu.VMEM((2, own, width), F32),
            pltpu.VMEM((radix, own, 2 * LANES), BF16),
            pltpu.VMEM((radix, own, 2 * LANES), BF16),
            pltpu.SemaphoreType.DMA((max(2, groups),)),
        ],
        compiler_params=pltpu.CompilerParams(vmem_limit_bytes=VMEM_LIMIT),
        name="middle",
    )(ids, tab["right_inverse"], tab["right_forward"], tab["twist_y"], *factors, mine, other)


def last_kernel(groups, rows, ids, back, twist, cosine, sine, weight, *refs):
    pieces = refs[: 2 * groups]
    source, receiver, image, data, field, halo, sems = refs[2 * groups :]
    z, core = ids[0], ids[2]
    half = data.shape[1] // 2
    copies, add = copier(sems)
    for e in range(groups):
        for h in (0, 1):
            piece = pieces[2 * e + h]
            for k in range(half):
                for part in (0, 1):
                    add(
                        piece.at[pl.ds((2 * k + part) * rows, rows), :],
                        data.at[z ^ e, (core ^ h) * half + k, part, pl.ds(0, rows), :],
                    )
            add(piece.at[pl.ds(2 * half * rows, 4 * half), :], halo.at[z ^ e, core ^ h])
    wait_all(copies)
    for g in range(groups):
        for h in (0, 1):
            for k in range(half):
                for part in (0, 1):
                    at = (2 * k + part) * 2
                    data[g, h * half + k, part, pl.ds(rows, 2), :] = halo[g, h, at : at + 2, :]
    total = jnp.zeros(image.shape, F32)
    for number in range(groups // 2):
        new = []
        for which, out in ((0, source), (1, receiver)):
            sign = 2.0 * which - 1.0

            def store(part, row, lane, value):
                field[part, row, lane] = value

            inverse_rows(
                lambda k, part, row: data[2 * number + which, k, part, row, :],
                rows + ROWS,
                back,
                twist,
                lambda row, lane: cosine[number, row, lane],
                lambda row, lane: sine[number, row, lane] * sign,
                store,
            )
            result = stencil(
                lambda part: field[part, pl.ds(0, rows), :],
                rows,
                lambda part, side: field[part, pl.ds(rows + side, 1), :],
                weight[number, pl.ds(0, rows), :],
                sign,
            )
            out[0, number] = result[0]
            out[1, number] = result[1]
        total = total + source[0, number] * receiver[0, number] + source[1, number] * receiver[1, number]
    image[...] = total


def last(ids, pieces, factors, tab, groups, rows):
    width = factors[0].shape[-1]
    radix = width // LANES
    half = radix // 2
    out = jax.ShapeDtypeStruct((2, groups // 2, rows, width), F32)
    vmem, hbm = pl.BlockSpec(memory_space=pltpu.VMEM), pl.BlockSpec(memory_space=pl.ANY)
    return pl.pallas_call(
        functools.partial(last_kernel, groups, rows),
        out_shape=(out, out, jax.ShapeDtypeStruct((rows, width), F32)),
        in_specs=[pl.BlockSpec(memory_space=pltpu.SMEM)] + [vmem] * 5 + [hbm] * (2 * groups),
        out_specs=(vmem, vmem, vmem),
        scratch_shapes=[
            pltpu.VMEM((groups, radix, 2, rows + ROWS, LANES), F32),
            pltpu.VMEM((2, rows + ROWS, width), F32),
            pltpu.VMEM((groups, 2, 4 * half, LANES), F32),
            pltpu.SemaphoreType.DMA((2 * groups * (2 * half + 1),)),
        ],
        compiler_params=pltpu.CompilerParams(vmem_limit_bytes=VMEM_LIMIT),
        name="last",
    )(ids, tab["right_inverse"], tab["twist_y"], *factors, *pieces)


def centered(position, length):
    shifted = jnp.where(position < length // 2, position, position - length)
    return shifted.astype(F32) * (2.0 * math.pi / length)


def column_filter(angular, sign, height, width, first_block, blocks):
    radix_x, radix_y = height // LANES, width // LANES
    inner = jnp.arange(LANES, dtype=jnp.int32)
    wave_x = centered(jnp.arange(radix_x, dtype=jnp.int32)[:, None] + radix_x * inner[None, :], height)
    wave_y = centered(first_block + jnp.arange(blocks, dtype=jnp.int32)[:, None] + radix_y * inner[None, :], width)
    wave_x = wave_x[None, :, :, None]
    wave_y = wave_y[:, None, None, :]
    argument = angular * angular - (wave_x * wave_x + wave_y * wave_y)
    radius = jnp.sqrt(jnp.abs(argument))
    travel = argument >= 0.0
    scale = 1.0 / (height * width)
    real = jnp.where(travel, jnp.cos(step_length * radius), jnp.exp(-step_length * radius)) * scale
    imag = sign * jnp.where(travel, jnp.sin(step_length * radius), 0.0) * scale
    return real, imag


def correction(speed, angular):
    phase = angular * step_length * (1.0 / speed - 1.0)
    return jnp.cos(phase), jnp.sin(phase), stencil_gain * (speed * speed - 1.0) * angular / omega_top


def local(source_field, receiver_field, velocity, slice_owner):
    freq_local, rows, width = source_field.shape[1:]
    strips = lax.axis_size("strip")
    planes = lax.axis_size("freq")
    height = rows * strips
    groups = 2 * freq_local
    members = strips // groups
    across = members // 2
    count = groups * across
    radix = width // LANES
    half = radix // 2
    freq_total = freq_local * planes
    me = lax.axis_index("strip")
    plane = lax.axis_index("freq")
    z, y, core = me // members, (me // 2) % across, me % 2
    ids = jnp.stack([z, y, core]).astype(jnp.int32)

    def swap(value, bit):
        return lax.ppermute(value, "strip", [(i, i ^ bit) for i in range(strips)])

    def swap_z(value, e):
        return swap(value, e * members)

    def swap_y(value, r):
        return swap(value, 2 * r)

    def swap_core(value):
        return swap(value, 1)

    def ahead_plane(value, k):
        return lax.ppermute(value, "freq", [(i, (i + k) % planes) for i in range(planes)])

    forward, inverse = point_tables()
    stack = lambda table: jnp.asarray(np.stack(halves(table)))
    both = lambda table: jnp.asarray(np.concatenate(halves(table)))
    tab = {
        "right_forward": stack(forward),
        "right_inverse": stack(inverse),
        "left_forward": both(forward.T),
        "left_inverse": both(inverse.T),
        "twist_y": jnp.asarray(twiddles(radix)),
        "twist_x": jnp.broadcast_to(
            jnp.asarray(twiddles(height // LANES))[..., None], (2, height // LANES, LANES, LANES)
        ),
    }

    slots = velocity.shape[0]
    shelf = jnp.stack([velocity] + [ahead_plane(velocity, k) for k in range(1, planes)])

    def own_slice(depth):
        number = slice_owner[depth]
        return lax.dynamic_slice(
            shelf,
            ((plane - number // slots) % planes, number % slots, 0, 0),
            (1, 1, rows, width),
        )[0, 0]

    speeds = [own_slice(depth) for depth in range(DEPTHS)]
    mid_speed = lax.all_gather(
        speeds[0],
        "strip",
        axis_index_groups=[[i for i in range(strips) if i % 2 == c] for c in (0, 1)],
    )
    edges = lax.all_gather(jnp.stack([jnp.stack([s[0], s[-1]]) for s in speeds]), "strip")
    one = jnp.ones((1, width), F32)
    above = [jnp.concatenate([one, edges[:-1, d, 1]]) for d in range(DEPTHS)]
    below = [jnp.concatenate([edges[1:, d, 0], one]) for d in range(DEPTHS)]

    keep, send = first_transform(ids, source_field, receiver_field, groups, tab)
    recv = swap_core(send)
    pieces = []
    for e in range(groups):
        message = jnp.stack([keep[e], recv[e]])
        pieces.append(swap_z(message, e) if e else message)
    full = []
    for e in range(groups):
        full.append(pieces[e])
        for r in range(1, across):
            full.append(swap_y(pieces[e], r))

    angular = omega_top * (plane * freq_local + z // 2 + 1).astype(F32) / freq_total
    sign = jnp.where(z % 2 == 0, -1.0, 1.0).astype(F32)
    filt = column_filter(angular, sign, height, width, core * half, half)

    mine, give = enter_columns(ids, full, filt, tab, groups, across)
    other = swap_core(give)
    beside = jnp.stack([above[0], below[0]], axis=1).reshape(count, 2, 2, width)
    beside = lax.dynamic_index_in_dim(beside, core, 1, keepdims=False).reshape(2 * count, width)
    tall = jnp.concatenate([mid_speed.reshape(count * rows, width), beside])
    cosine, sine, weight = correction(tall, angular)
    mine, give, near, far = middle(ids, mine, other, (cosine, sign * sine, weight), tab, groups, across)

    other = swap_core(give)
    outs = leave_columns(ids, mine, other, filt, tab, groups, across)
    arrived = []
    for e in range(groups):
        kept, given = outs[2 * e], outs[2 * e + 1]
        if e:
            given, kept = swap_z(given, e), swap_z(kept, e)
        arrived += [kept, swap_core(given)]

    across_freq = swap_z(far, 1)
    image = near[0] * across_freq[0] + near[1] * across_freq[1]

    def spread(value):
        wide = width // planes
        part = lambda k: lax.dynamic_slice_in_dim(value, ((plane + k) % planes) * wide, wide, axis=value.ndim - 1)
        total = part(0)
        for k in range(1, planes):
            total = total + ahead_plane(part(k), k)
        return total

    image = spread(image)
    first_image = lax.dynamic_index_in_dim(image, z // 2, 0, keepdims=False)
    for d in range(1, groups // 2):
        piece = lax.dynamic_index_in_dim(image, (z // 2) ^ d, 0, keepdims=False)
        first_image = first_image + swap_z(piece, 2 * d)

    numbers = jnp.arange(freq_local, dtype=jnp.int32) + plane * freq_local
    angulars = (omega_top * (numbers + 1).astype(F32) / freq_total)[:, None, None]
    ends = [lax.dynamic_index_in_dim(side[1], me, 0) for side in (above, below)]
    spare = jnp.ones((ROWS - 2, width), F32)
    tall = jnp.concatenate([speeds[1]] + ends + [spare])
    source_out, receiver_out, last_image = last(ids, arrived, correction(tall[None], angulars), tab, groups, rows)
    depth_image = jnp.stack([first_image, spread(last_image)])
    return (depth_image, source_out, receiver_out)


def solution(mesh):
    return jax.shard_map(
        local,
        mesh=mesh,
        in_specs=(
            P(None, "freq", "strip", None),
            P(None, "freq", "strip", None),
            P("freq", "strip", None),
            P(),
        ),
        out_specs=(
            P(None, "strip", "freq"),
            P(None, "freq", "strip", None),
            P(None, "freq", "strip", None),
        ),
        check_vma=False,
    )
```

```python
import functools
import math

import jax
import jax.numpy as jnp
import numpy as np
from jax import lax
from jax.experimental import pallas as pl
from jax.experimental.pallas import tpu as pltpu
from jax.sharding import PartitionSpec as P

DEPTHS = 2

step_length = 0.15
omega_top = 1.2
stencil_gain = 0.05
stencil_damping = 0.1

LANES = 128
ROWS = 16
VMEM_LIMIT = 56 * 1024 * 1024
ANY = pl.BlockSpec(memory_space=pl.ANY)
VMEM = pl.BlockSpec(memory_space=pltpu.VMEM)
SMEM = pl.BlockSpec(memory_space=pltpu.SMEM)
F32 = jnp.float32
BF16 = jnp.bfloat16


def halves(table):
    table = np.asarray(table, np.float32)
    high = table.astype(jnp.bfloat16)
    low = (table - high.astype(np.float32)).astype(jnp.bfloat16)
    return high, low


def point_tables():
    index = np.arange(LANES)
    angle = 2.0 * np.pi * (index[:, None] * index[None, :] % LANES) / LANES
    cosine, sine = np.cos(angle), np.sin(angle)
    forward = np.block([[cosine, -sine], [sine, cosine]])
    return forward, forward.T


def twiddles(radix):
    length = radix * LANES
    angle = 2.0 * np.pi * (np.arange(radix)[:, None] * np.arange(LANES)[None, :]) / length
    return np.stack([np.cos(angle), -np.sin(angle)]).astype(np.float32)


def small_dft(real, imag, sign):
    count = len(real)
    if count == 1:
        return list(real), list(imag)
    even = small_dft(real[0::2], imag[0::2], sign)
    odd = small_dft(real[1::2], imag[1::2], sign)
    half = count // 2
    top_real, top_imag, low_real, low_imag = [], [], [], []
    for k in range(half):
        o_re, o_im = odd[0][k], odd[1][k]
        if k == 0:
            t_re, t_im = o_re, o_im
        elif 4 * k == count:
            t_re, t_im = (-o_im, o_re) if sign > 0 else (o_im, -o_re)
        elif 8 * k == count:
            h = math.sqrt(0.5)
            t_re, t_im = ((o_re - o_im) * h, (o_im + o_re) * h) if sign > 0 else ((o_re + o_im) * h, (o_im - o_re) * h)
        elif 8 * k == 3 * count:
            h = math.sqrt(0.5)
            t_re, t_im = ((-o_re - o_im) * h, (o_re - o_im) * h) if sign > 0 else ((o_im - o_re) * h, (-o_re - o_im) * h)
        else:
            w_re, w_im = math.cos(2 * math.pi * k / count), sign * math.sin(2 * math.pi * k / count)
            t_re, t_im = o_re * w_re - o_im * w_im, o_re * w_im + o_im * w_re
        top_real.append(even[0][k] + t_re)
        top_imag.append(even[1][k] + t_im)
        low_real.append(even[0][k] - t_re)
        low_imag.append(even[1][k] - t_im)
    return top_real + low_real, top_imag + low_imag


def parts(value):
    high = value.astype(BF16)
    return high, (value - high.astype(F32)).astype(BF16)


def dot(left, right):
    return jnp.dot(left, right, preferred_element_type=F32)


def dot_right(high, low, table):
    return dot(high, table[0]) + dot(low, table[0]) + dot(high, table[1])


def dot_left(both, data_high, data_low):
    size = both.shape[0] // 2
    first = dot(both[...], data_high)
    return first[:size] + first[size:] + dot(both[:size], data_low)


def lanes(k, count=1):
    return slice(k * LANES, (k + count) * LANES)


def turned(re, im, twist, k, row, back):
    if k == 0:
        return re, im
    c, s = twist[0, k, row, :], twist[1, k, row, :]
    if back:
        return re * c + im * s, im * c - re * s
    return re * c - im * s, re * s + im * c


def forward_into(load, row, twist, high, low, index):
    radix = twist.shape[1]
    real, imag = zip(*[load(a) for a in range(radix)])
    real, imag = small_dft(list(real), list(imag), -1)
    for k in range(radix):
        pair = turned(real[k], imag[k], twist, k, slice(0, 1), False)
        for part in (0, 1):
            h, l = parts(pair[part])
            high[index(k) + (row, lanes(part))] = h
            low[index(k) + (row, lanes(part))] = l


def inverse_tiles(load, size, table, twist):
    radix = twist.shape[1]
    data = jnp.concatenate([jnp.concatenate([load(k, 0), load(k, 1)], axis=1) for k in range(radix)], axis=0)
    result = dot_right(*parts(data), table)
    real, imag = [], []
    for k in range(radix):
        row = slice(k * size, (k + 1) * size)
        re, im = turned(result[row, lanes(0)], result[row, lanes(1)], twist, k, slice(0, 1), True)
        real.append(re)
        imag.append(im)
    return small_dft(real, imag, 1)


class Copies:
    def __init__(self, sems):
        self.sems, self.used = sems, 0

    def __call__(self, *pairs):
        made = []
        for source, target in pairs:
            made.append(pltpu.make_async_copy(source, target, self.sems.at[self.used]))
            self.used += 1
        for copy in made:
            copy.start()
        return made


def done(copies):
    for copy in copies:
        copy.wait()


def call(kernel, name, out_shape, in_specs, out_specs, scratch, flops, moved, args):
    return pl.pallas_call(
        kernel,
        out_shape=out_shape,
        in_specs=in_specs,
        out_specs=out_specs,
        scratch_shapes=scratch,
        compiler_params=pltpu.CompilerParams(vmem_limit_bytes=VMEM_LIMIT),
        cost_estimate=pl.CostEstimate(flops=flops, bytes_accessed=moved, transcendentals=0),
        name=name,
    )(*args)


def first_kernel(offsets, final, ids, source, receiver, table, twist, *refs):
    high, low, given, out, sems = refs[-5:]
    messages = refs[:-5]
    z, core = ids[0], ids[2]
    radix = twist.shape[1]
    half = radix // 2
    rows = source.shape[2]
    for e, offset in enumerate(offsets):
        field = z ^ offset
        which, number = lax.rem(field, 2), lax.div(field, 2)
        for kind, ref in ((0, source), (1, receiver)):

            @pl.when(which == kind)
            def start(e=e, ref=ref, number=number):
                pltpu.make_async_copy(ref.at[:, number], given.at[e], sems.at[e]).start()

    leaving, used = [], len(offsets)
    place = 0
    for e, offset in enumerate(offsets):
        pltpu.make_async_copy(source.at[:, 0], given.at[e], sems.at[e]).wait()

        def chunk(t, carry, e=e):
            row = pl.ds(pl.multiple_of(t * ROWS, ROWS), ROWS)
            forward_into(
                lambda a: (given[e, 0, row, lanes(a)], given[e, 1, row, lanes(a)]), row, twist, high, low, lambda k: (e, k)
            )
            return carry

        lax.fori_loop(0, rows // ROWS, chunk, 0)
        for slot, start in ((0, core * half), (1, (1 - core) * half)):
            h = high[e, pl.ds(start, half)].reshape(half * rows, 2 * LANES)
            l = low[e, pl.ds(start, half)].reshape(half * rows, 2 * LANES)
            result = dot_right(h, l, table)
            for k in range(half):
                for part in (0, 1):
                    at = (slot * half + k) * 2 + part
                    out[e, at * rows : (at + 1) * rows, :] = result[k * rows : (k + 1) * rows, lanes(part)]
        moves = []
        if offset == final:
            for p in range(half // 2):
                for slot in (0, 1):
                    moves.append(
                        (
                            out.at[e, pl.ds((slot * half + 2 * p) * 2 * rows, 4 * rows)],
                            messages[place].at[pl.ds(slot * 4 * rows, 4 * rows)],
                        )
                    )
                place += 1
        else:
            moves.append((out.at[e], messages[place]))
            place += 1
        for source_part, target in moves:
            copy = pltpu.make_async_copy(source_part, target, sems.at[used])
            copy.start()
            leaving.append(copy)
            used += 1
    done(leaving)


def first_transform(ids, source, receiver, offsets, final, tab):
    rows, width = source.shape[2:]
    radix = width // LANES
    tall = 2 * radix * rows
    shapes = []
    for offset in offsets:
        if offset == final:
            shapes += [jax.ShapeDtypeStruct((8 * rows, LANES), F32)] * (radix // 4)
        else:
            shapes.append(jax.ShapeDtypeStruct((tall, LANES), F32))
    count = len(offsets)
    return call(
        functools.partial(first_kernel, offsets, final),
        "first_transform",
        tuple(shapes),
        [SMEM, ANY, ANY, VMEM, VMEM],
        (ANY,) * len(shapes),
        [
            pltpu.VMEM((count, radix, rows, 2 * LANES), BF16),
            pltpu.VMEM((count, radix, rows, 2 * LANES), BF16),
            pltpu.VMEM((count, 2, rows, width), F32),
            pltpu.VMEM((count, tall, LANES), F32),
            pltpu.SemaphoreType.DMA((count + 2 * len(shapes),)),
        ],
        count * 1000000000,
        count * 1000000,
        (ids, source, receiver, tab["right_forward"], tab["twist_y"]),
    )


def shift_pair(pair, rows, data, filt_re, filt_im, ahead, back, twist, high, low, line):
    radix = twist.shape[1]
    per = rows // ROWS

    def spot(k, part, a, t):
        index = a * (LANES // ROWS) + t
        block, inner = lax.div(index, per), lax.rem(index, per)
        start = pl.multiple_of((2 * k + part) * rows + inner * ROWS, ROWS)
        return lax.div(block, 2), lax.rem(block, 2), pl.ds(start, ROWS)

    def fold(t, carry):
        off = pl.multiple_of(t * ROWS, ROWS)
        row = pl.ds(off, ROWS)
        for kk in (0, 1):
            real, imag = ([data[spot(pair + kk, part, a, t)] for a in range(radix)] for part in (0, 1))
            real, imag = small_dft(real, imag, -1)
            for k in range(radix):
                turn_pair = turned(real[k], imag[k], twist, k, row, False)
                for part in (0, 1):
                    h, l = parts(turn_pair[part])
                    high[k, pl.ds(part * LANES + off, ROWS), lanes(kk)] = h
                    low[k, pl.ds(part * LANES + off, ROWS), lanes(kk)] = l
        return carry

    lax.fori_loop(0, LANES // ROWS, fold, 0)

    def spectral(k, carry):
        value = dot_left(ahead, high[k], low[k])
        re, im = value[:LANES], value[LANES:]
        fr = jnp.concatenate([filt_re[pair, k], filt_re[pair + 1, k]], axis=1)
        fi = jnp.concatenate([filt_im[pair, k], filt_im[pair + 1, k]], axis=1)
        both = jnp.concatenate([re * fr - im * fi, re * fi + im * fr], axis=0)
        h, l = parts(both)
        line[k] = dot_left(back, h, l)
        return carry

    lax.fori_loop(0, radix, spectral, 0, unroll=4)

    def unfold(t, carry):
        off = pl.multiple_of(t * ROWS, ROWS)
        row = pl.ds(off, ROWS)
        for kk in (0, 1):
            real, imag = [], []
            for k in range(radix):
                re = line[k, pl.ds(off, ROWS), lanes(kk)]
                im = line[k, pl.ds(LANES + off, ROWS), lanes(kk)]
                re, im = turned(re, im, twist, k, row, True)
                real.append(re)
                imag.append(im)
            both = small_dft(real, imag, 1)
            for part in (0, 1):
                for a in range(radix):
                    data[spot(pair + kk, part, a, t)] = both[part][a]
        return carry

    lax.fori_loop(0, LANES // ROWS, unfold, 0)


def outer_rows(rows, half, data):
    count = data.shape[0]
    for b in range(2 * count):
        for k in range(half):
            for part in (0, 1):
                base = (2 * k + part) * rows
                at = 2 * half * rows + (2 * k + part) * 2
                for side, beside, row in ((0, b - 1, base + rows - 1), (1, b + 1, base)):
                    if 0 <= beside < 2 * count:
                        value = data[beside // 2, beside % 2, row : row + 1, :]
                    else:
                        value = jnp.zeros((1, LANES), F32)
                    data[b // 2, b % 2, at + side : at + side + 1, :] = value


def enter_kernel(groups, across, rows, ids, filt_re, filt_im, ahead, back, twist, *refs):
    keep, send, data, fre, fim, tw, high, low, line, sems = refs[-10:]
    pieces = refs[:-10]
    z, y, core = ids[0], ids[1], ids[2]
    half = fre.shape[0]
    pairs = half // 2
    copies = Copies(sems)
    first = copies((twist, tw))
    arrivals = []
    for p in range(pairs):
        moves = []
        at = 0
        for e in range(groups):
            split = e == groups - 1
            for r in range(across):
                block = (z ^ e) * across + (y ^ r)
                for h in (0, 1):
                    piece = pieces[at + (p if split else 0)]
                    at += pairs if split else 1
                    start = h * 4 * rows if split else (h * half + 2 * p) * 2 * rows
                    moves.append(
                        (
                            piece.at[pl.ds(start, 4 * rows)],
                            data.at[block, core ^ h, pl.ds(4 * p * rows, 4 * rows)],
                        )
                    )
        moves += [(a.at[pl.ds(2 * p, 2)], b.at[pl.ds(2 * p, 2)]) for a, b in ((filt_re, fre), (filt_im, fim))]
        arrivals.append(copies(*moves))
    done(first)
    leaving = []
    for p in range(pairs):
        done(arrivals[p])
        shift_pair(2 * p, rows, data, fre, fim, ahead, back, tw, high, low, line)
        lot = pl.ds(4 * p * rows, 4 * rows)
        leaving += copies(*[(data.at[:, par, lot], out.at[:, lot]) for out, par in ((send, 1 - core), (keep, core))])
    outer_rows(rows, half, data)
    lot = pl.ds(2 * half * rows, 4 * half)
    leaving += copies(*[(data.at[:, par, lot], out.at[:, lot]) for out, par in ((send, 1 - core), (keep, core))])
    done(leaving)


def leave_kernel(groups, across, rows, ids, filt_re, filt_im, ahead, back, twist, mine, other, *refs):
    data, fre, fim, tw, high, low, line, sems = refs[-8:]
    outs = refs[:-8]
    z, y, core = ids[0], ids[1], ids[2]
    half = fre.shape[0]
    pairs = half // 2
    copies = Copies(sems)
    first = copies((twist, tw))
    arrivals = []
    for p in range(pairs):
        lot = pl.ds(4 * p * rows, 4 * rows)
        moves = [(mine.at[:, lot], data.at[:, core, lot]), (other.at[:, lot], data.at[:, 1 - core, lot])]
        moves += [(a.at[pl.ds(2 * p, 2)], b.at[pl.ds(2 * p, 2)]) for a, b in ((filt_re, fre), (filt_im, fim))]
        arrivals.append(copies(*moves))
    done(first)
    for p in range(pairs):
        done(arrivals[p])
        shift_pair(2 * p, rows, data, fre, fim, ahead, back, tw, high, low, line)
    outer_rows(rows, half, data)
    moves = []
    for e in range(groups):
        for h in (0, 1):
            moves.append((data.at[(z ^ e) * across + y, core ^ h], outs[2 * e + h]))
    done(copies(*moves))


def column_scratch(half, count, rows, copies):
    radix = 2 * count * rows // LANES
    return [
        pltpu.VMEM((count, 2, 2 * half * rows + 4 * half, LANES), F32),
        pltpu.VMEM((half, radix, LANES, LANES), F32),
        pltpu.VMEM((half, radix, LANES, LANES), F32),
        pltpu.VMEM((2, radix, LANES, LANES), F32),
        pltpu.VMEM((radix, 2 * LANES, 2 * LANES), BF16),
        pltpu.VMEM((radix, 2 * LANES, 2 * LANES), BF16),
        pltpu.VMEM((radix, 2 * LANES, 2 * LANES), F32),
        pltpu.SemaphoreType.DMA((copies,)),
    ]


def enter_columns(ids, pieces, filt, tab, groups, across, rows, half):
    count = groups * across
    out = jax.ShapeDtypeStruct((count, 2 * half * rows + 4 * half, LANES), F32)
    pairs = half // 2
    return call(
        functools.partial(enter_kernel, groups, across, rows),
        "enter_columns",
        (out, out),
        [SMEM, ANY, ANY, VMEM, VMEM, ANY] + [ANY] * len(pieces),
        (ANY, ANY),
        column_scratch(half, count, rows, 1 + pairs * (2 * count + 4) + 2),
        8000000000,
        8000000,
        (ids, *filt, tab["left_forward"], tab["left_inverse"], tab["twist_x"], *pieces),
    )


def leave_columns(ids, mine, other, filt, tab, groups, across, rows, half):
    count = groups * across
    out = jax.ShapeDtypeStruct((2 * half * rows + 4 * half, LANES), F32)
    return call(
        functools.partial(leave_kernel, groups, across, rows),
        "leave_columns",
        (out,) * (2 * groups),
        [SMEM, ANY, ANY, VMEM, VMEM, ANY, ANY, ANY],
        (ANY,) * (2 * groups),
        column_scratch(half, count, rows, 1 + 2 * half + 2 * groups),
        8000000000,
        8000000,
        (ids, *filt, tab["left_forward"], tab["left_inverse"], tab["twist_x"], mine, other),
    )


def turn(square):
    cosine, ratio = 1.0, 1.0
    for n in (4, 3, 2, 1):
        cosine = 1.0 - cosine * square * (1.0 / ((2 * n - 1) * (2 * n)))
        ratio = 1.0 - ratio * square * (1.0 / ((2 * n) * (2 * n + 1)))
    return cosine, ratio


def correction(speed, angular, sign):
    phase = (sign * step_length) * angular * (1.0 / speed - 1.0)
    cosine, ratio = turn(phase * phase)
    return cosine, ratio * phase, stencil_gain * (speed * speed - 1.0) * angular / omega_top


def stencil(field, halo, weight, sign, store):
    radix, weigh = weight
    shape = field(0, 0).shape
    line = lax.broadcasted_iota(jnp.int32, shape, 0)
    place = lax.broadcasted_iota(jnp.int32, shape, 1)
    top, bottom = line == 0, line == shape[0] - 1
    left, right = place == 0, place == LANES - 1
    zero = jnp.zeros(shape, F32)
    before = [zero, zero]
    for a in range(radix):
        center, bent = [], []
        for part in (0, 1):
            value = field(part, a)
            ahead = pltpu.roll(value, 1, axis=1)
            west = jnp.where(left, before[part], ahead)
            before[part] = ahead
            follow = pltpu.roll(field(part, a + 1), LANES - 1, axis=1) if a + 1 < radix else zero
            east = jnp.where(right, follow, pltpu.roll(value, LANES - 1, axis=1))
            north = jnp.where(top, halo(part, 0, a), pltpu.roll(value, 1, axis=0))
            south = jnp.where(bottom, halo(part, 1, a), pltpu.roll(value, shape[0] - 1, axis=0))
            center.append(value)
            bent.append((north + south) + (west + east) - 4.0 * value)
        heavy = weigh(a)
        twist, damp = heavy * sign, heavy * stencil_damping
        store(0, a, center[0] + damp * bent[0] - twist * bent[1])
        store(1, a, center[1] + damp * bent[1] + twist * bent[0])


def middle_kernel(groups, across, rows, ids, back, ahead, twist, halo_cos, halo_sin, cosine, sine, weight, mine, other, *refs):
    keep, send, near, far, data, halo, cos, sin, wei, field, edge, fresh, high, low, out, block_sems, sems = refs
    z, y, core = ids[0], ids[1], ids[2]
    which = lax.rem(z, 2)
    sign = jnp.where(which == 0, -1.0, 1.0).astype(F32)
    count = groups * across
    radix = twist.shape[1]
    half = radix // 2
    own, outer = pl.ds(0, 2 * half * rows), pl.ds(2 * half * rows, 4 * half)
    copies = Copies(sems)
    first = copies((mine.at[:, outer], halo.at[core]), (other.at[:, outer], halo.at[1 - core]))

    def arrivals(i):
        pairs = (
            (mine.at[i, own], data.at[core, i]),
            (other.at[i, own], data.at[1 - core, i]),
            (cosine.at[i], cos.at[i]),
            (sine.at[i], sin.at[i]),
            (weight.at[i], wei.at[i]),
        )
        return [pltpu.make_async_copy(a, b, block_sems.at[i, n]) for n, (a, b) in enumerate(pairs)]

    def launch(i, carry):
        for copy in arrivals(i):
            copy.start()
        return carry

    lax.fori_loop(0, count, launch, 0)
    done(first)

    def halo_rows(k, part):
        at = (2 * (k % half) + part) * 2
        return jnp.concatenate([halo[k // half, i, at : at + 2, :] for i in range(count)], axis=0)

    real, imag = inverse_tiles(halo_rows, 2 * count, back, twist)
    for a in range(radix):
        c, s = halo_cos[a], halo_sin[a]
        edge[0, a] = real[a] * c - imag[a] * s
        edge[1, a] = real[a] * s + imag[a] * c

    def departures(i):
        pairs = ((out.at[1, i], send.at[i]), (out.at[0, i], keep.at[i]))
        return [pltpu.make_async_copy(a, b, block_sems.at[i, n]) for n, (a, b) in enumerate(pairs)]

    def block(i, carry):
        done(arrivals(i))
        real, imag = inverse_tiles(
            lambda k, part: data[k // half, i, (2 * (k % half) + part) * rows : (2 * (k % half) + part + 1) * rows, :],
            rows,
            back,
            twist,
        )
        for a in range(radix):
            c, s = cos[i, a], sin[i, a]
            field[0, a] = real[a] * c - imag[a] * s
            field[1, a] = real[a] * s + imag[a] * c

        def store(part, a, value):
            fresh[part, i, :, lanes(a)] = value

        stencil(
            lambda part, a: field[part, a],
            lambda part, side, a: edge[part, a, pl.ds(2 * i + side, 1), :],
            (radix, lambda a: wei[i, a]),
            sign,
            store,
        )

        def fold(t, carry):
            row = pl.ds(pl.multiple_of(t * ROWS, ROWS), ROWS)
            forward_into(
                lambda a: (fresh[0, i, row, lanes(a)], fresh[1, i, row, lanes(a)]), row, twist, high, low, lambda k: (k,)
            )
            return carry

        lax.fori_loop(0, rows // ROWS, fold, 0)
        for slot, start in ((1, (1 - core) * half), (0, core * half)):
            h = high[pl.ds(start, half)].reshape(half * rows, 2 * LANES)
            l = low[pl.ds(start, half)].reshape(half * rows, 2 * LANES)
            result = dot_right(h, l, ahead)
            for k in range(half):
                for part in (0, 1):
                    at = 2 * k + part
                    out[slot, i, at * rows : (at + 1) * rows, :] = result[k * rows : (k + 1) * rows, lanes(part)]
        for copy in departures(i):
            copy.start()
        return carry

    lax.fori_loop(0, count, block, 0)
    leaving = []
    for target, parity in ((far, 1 - which), (near, which)):
        for t in range(groups // 2):
            leaving += copies((fresh.at[:, (parity + 2 * t) * across + y], target.at[:, t]))

    def settle(i, carry):
        done(departures(i))
        return carry

    lax.fori_loop(0, count, settle, 0)
    done(leaving)


def middle(ids, mine, other, factors, tab, groups, across, rows, half):
    count = groups * across
    radix = 2 * half
    width = radix * LANES
    out = jax.ShapeDtypeStruct((count, 2 * half * rows, LANES), F32)
    image = jax.ShapeDtypeStruct((2, groups // 2, rows, width), F32)
    cosine, sine, weight, halo_cos, halo_sin = factors
    blocks = pltpu.VMEM((count, radix, rows, LANES), F32)
    return call(
        functools.partial(middle_kernel, groups, across, rows),
        "middle",
        (out, out, image, image),
        [SMEM] + [VMEM] * 5 + [ANY] * 5,
        (ANY,) * 4,
        [
            pltpu.VMEM((2, count, 2 * half * rows, LANES), F32),
            pltpu.VMEM((2, count, 4 * half, LANES), F32),
            blocks,
            blocks,
            blocks,
            pltpu.VMEM((2, radix, rows, LANES), F32),
            pltpu.VMEM((2, radix, 2 * count, LANES), F32),
            pltpu.VMEM((2, count, rows, width), F32),
            pltpu.VMEM((radix, rows, 2 * LANES), BF16),
            pltpu.VMEM((radix, rows, 2 * LANES), BF16),
            pltpu.VMEM((2, count, 2 * half * rows, LANES), F32),
            pltpu.SemaphoreType.DMA((count, 5)),
            pltpu.SemaphoreType.DMA((2 + groups,)),
        ],
        16000000000,
        10000000,
        (
            ids,
            tab["right_inverse"],
            tab["right_forward"],
            tab["twist_y"],
            halo_cos,
            halo_sin,
            cosine,
            sine,
            weight,
            mine,
            other,
        ),
    )


def prepare_kernel(groups, across, ids, scales, *refs):
    number = across
    pieces, others = refs[:number], refs[number : 2 * number]
    cosine, sine, weight, halo_cos, halo_sin, speed, lasts, firsts, sems = refs[2 * number :]
    z, y, core = ids[0], ids[1], ids[2]
    count, radix, rows, _ = speed.shape
    one = jnp.ones((radix, 8, LANES), F32)
    lasts[0] = one
    firsts[count] = one
    copies = Copies(sems)
    moves, beside = [], []
    for r in range(across):
        for n, e in enumerate(gather_order(groups)):
            block = (z ^ e) * across + (y ^ r)
            moves.append((pieces[r].at[n], speed.at[block]))
            beside.append((others[r].at[n, :, pl.ds(rows - 8, 8)], lasts.at[block + 1 - core]))
            beside.append((others[r].at[n, :, pl.ds(0, 8)], firsts.at[block + 1 - core]))
    moves, beside = copies(*moves), copies(*beside)
    done(moves)

    def chunk(i, carry):
        for a in range(radix):
            cosine[i, a], sine[i, a], weight[i, a] = correction(speed[i, a], scales[0], scales[1])
        return carry

    lax.fori_loop(0, count, chunk, 0)
    done(beside)
    for a in range(radix):
        rows_beside = []
        for i in range(count):
            rows_beside += [lasts[i, a, 7:8, :], firsts[i + 1, a, 0:1, :]]
        halo_cos[a], halo_sin[a], _ = correction(jnp.concatenate(rows_beside, axis=0), scales[0], scales[1])


def prepare(ids, scales, pieces, others, groups, across):
    _, radix, rows, _ = pieces[0].shape
    count = groups * across
    out = jax.ShapeDtypeStruct((count, radix, rows, LANES), F32)
    halo = jax.ShapeDtypeStruct((radix, 2 * count, LANES), F32)
    return call(
        functools.partial(prepare_kernel, groups, across),
        "prepare",
        (out, out, out, halo, halo),
        [SMEM] * 2 + [ANY] * (2 * len(pieces)),
        (VMEM,) * 5,
        [
            pltpu.VMEM((count, radix, rows, LANES), F32),
            pltpu.VMEM((count + 1, radix, 8, LANES), F32),
            pltpu.VMEM((count + 1, radix, 8, LANES), F32),
            pltpu.SemaphoreType.DMA((3 * len(pieces) * groups,)),
        ],
        4000000000,
        8000000,
        (ids, scales, *pieces, *others),
    )


def last_kernel(groups, rows, ids, angulars, back, twist, speed, beside, *refs):
    source, receiver, image, data, field, edge, turns, sems = refs[-8:]
    pieces = refs[:-8]
    z, core = ids[0], ids[2]
    radix = twist.shape[1]
    half = radix // 2
    copies = Copies(sems)
    arrivals = copies(
        *[(pieces[2 * e + h], data.at[z ^ e, core ^ h]) for e in range(groups) for h in (0, 1)]
    )
    done(arrivals)

    def halo_rows(k, part):
        at = 2 * half * rows + (2 * (k % half) + part) * 2
        return jnp.concatenate(
            [data[g, k // half, at : at + 2, :] for g in range(groups)] + [jnp.zeros((tall - 2 * groups, LANES), F32)], axis=0
        )

    tall = -(-2 * groups // ROWS) * ROWS
    real, imag = inverse_tiles(halo_rows, tall, back, twist)
    for a in range(radix):
        for g in range(groups):
            c, s, _ = correction(beside[:, lanes(a)], angulars[g // 2], 2.0 * (g % 2) - 1.0)
            pair = slice(2 * g, 2 * g + 2)
            edge[0, a, pair, :] = real[a][pair] * c - imag[a][pair] * s
            edge[1, a, pair, :] = real[a][pair] * s + imag[a][pair] * c
    for number in range(groups // 2):
        for a in range(radix):
            turns[0, a], turns[1, a], turns[2, a] = correction(speed[:, lanes(a)], angulars[number], 1.0)
        for which, out in ((0, source), (1, receiver)):
            sign = 2.0 * which - 1.0
            g = 2 * number + which
            real, imag = inverse_tiles(
                lambda k, part: data[g, k // half, (2 * (k % half) + part) * rows : (2 * (k % half) + part + 1) * rows, :],
                rows,
                back,
                twist,
            )
            for a in range(radix):
                c, s = turns[0, a], turns[1, a] * sign
                field[0, a] = real[a] * c - imag[a] * s
                field[1, a] = real[a] * s + imag[a] * c

            def store(part, a, value):
                out[part, number, :, lanes(a)] = value

            stencil(
                lambda part, a: field[part, a],
                lambda part, side, a: edge[part, a, 2 * g + side : 2 * g + side + 1, :],
                (radix, lambda a: turns[2, a]),
                sign,
                store,
            )
    for a in range(radix):
        total = jnp.zeros((rows, LANES), F32)
        for number in range(groups // 2):
            for part in (0, 1):
                total = total + source[part, number, :, lanes(a)] * receiver[part, number, :, lanes(a)]
        image[:, lanes(a)] = total


def last(ids, angulars, speed, beside, pieces, tab, groups):
    rows, width = speed.shape
    radix = width // LANES
    out = jax.ShapeDtypeStruct((2, groups // 2, rows, width), F32)
    return call(
        functools.partial(last_kernel, groups, rows),
        "last",
        (out, out, jax.ShapeDtypeStruct((rows, width), F32)),
        [SMEM] * 2 + [VMEM] * 4 + [ANY] * (2 * groups),
        (VMEM,) * 3,
        [
            pltpu.VMEM((groups, 2, radix * rows + 2 * radix, LANES), F32),
            pltpu.VMEM((2, radix, rows, LANES), F32),
            pltpu.VMEM((2, radix, 2 * groups, LANES), F32),
            pltpu.VMEM((3, radix, rows, LANES), F32),
            pltpu.SemaphoreType.DMA((2 * groups,)),
        ],
        8000000000,
        8000000,
        (ids, angulars, tab["right_inverse"], tab["twist_y"], speed, beside, *pieces),
    )


def gather_order(groups):
    order = [0]
    for bit in bits(groups):
        order += [e ^ bit for e in order]
    return order


def after(value, *others):
    return lax.optimization_barrier((value, others))[0]


def bits(count):
    return [1 << n for n in reversed(range(count.bit_length() - 1))]


def centered(position, length):
    shifted = jnp.where(position < length // 2, position, position - length)
    return shifted.astype(F32) * (2.0 * math.pi / length)


def column_filter(angular, sign, height, width, first_block, blocks):
    radix_x, radix_y = height // LANES, width // LANES
    inner = jnp.arange(LANES, dtype=jnp.int32)
    wave_x = centered(jnp.arange(radix_x, dtype=jnp.int32)[:, None] + radix_x * inner[None, :], height)
    wave_y = centered(first_block + jnp.arange(blocks, dtype=jnp.int32)[:, None] + radix_y * inner[None, :], width)
    wave_x = wave_x[None, :, :, None]
    wave_y = wave_y[:, None, None, :]
    argument = angular * angular - (wave_x * wave_x + wave_y * wave_y)
    radius = step_length * jnp.sqrt(jnp.abs(argument))
    travel = argument >= 0.0
    scale = 1.0 / (height * width)
    cosine, ratio = turn(jnp.where(travel, radius * radius, 0.0))
    real = jnp.where(travel, cosine, jnp.exp(-radius)) * scale
    imag = jnp.where(travel, ratio * radius, 0.0) * (sign * scale)
    return real, imag


def local(source_field, receiver_field, velocity, slice_owner):
    freq_local, rows, width = source_field.shape[1:]
    strips = lax.axis_size("strip")
    planes = lax.axis_size("freq")
    height = rows * strips
    groups = 2 * freq_local
    members = strips // groups
    across = members // 2
    radix = width // LANES
    half = radix // 2
    freq_total = freq_local * planes
    me = lax.axis_index("strip")
    plane = lax.axis_index("freq")
    z, y, core = me // members, (me // 2) % across, me % 2
    ids = jnp.stack([z, y, core, plane]).astype(jnp.int32)

    def swap(value, bit):
        return lax.ppermute(value, "strip", [(i, i ^ bit) for i in range(strips)])

    def swap_z(value, e):
        return swap(value, e * members)

    def swap_y(value, r):
        return swap(value, 2 * r)

    def swap_core(value):
        return swap(value, 1)

    def ahead_plane(value, k):
        return lax.ppermute(value, "freq", [(i, (i + k) % planes) for i in range(planes)])

    forward, inverse = point_tables()
    stack = lambda table: jnp.asarray(np.stack(halves(table)))
    both = lambda table: jnp.asarray(np.concatenate(halves(table)))
    tab = {
        "right_forward": stack(forward),
        "right_inverse": stack(inverse),
        "left_forward": both(forward.T),
        "left_inverse": both(inverse.T),
        "twist_y": jnp.asarray(twiddles(radix)[:, :, None, :]),
        "twist_x": jnp.asarray(np.repeat(twiddles(height // LANES)[..., None], LANES, axis=-1)),
    }

    slots = velocity.shape[0]
    shelf = jnp.stack([velocity] + [ahead_plane(velocity, k) for k in range(1, planes)])

    def own_slice(depth):
        number = slice_owner[depth]
        return lax.dynamic_slice(
            shelf,
            ((plane - number // slots) % planes, number % slots, 0, 0),
            (1, 1, rows, width),
        )[0, 0]

    speeds = [own_slice(depth) for depth in range(DEPTHS)]

    final, top = groups - 1, groups // 2
    messages = {}
    order = [top, 0] + [e for e in range(1, final) if e != top] + [final]
    made = list(first_transform(ids, source_field, receiver_field, order, final, tab))
    for e in order:
        messages[e] = [made.pop(0) for _ in range(half // 2 if e == final else 1)]
    pieces, full = {0: messages[0]}, {}

    def share(e, *waits):
        ready = [after(piece, wait) for piece, wait in zip(pieces[e], waits)] if waits else pieces[e]
        mine = [pieces[e]] + [[] for r in range(1, across)]
        for piece in ready:
            sent = [swap_y(after(piece, mine[r][-1:]), r) for r in range(1, across)]
            for r in range(1, across):
                mine[r].append(sent[r - 1])
        full[e] = [lot for own in mine for lot in (own, [swap_core(piece) for piece in own])]

    angular = omega_top * (plane * freq_local + z // 2 + 1).astype(F32) / freq_total
    sign = jnp.where(z % 2 == 0, -1.0, 1.0).astype(F32)
    filt = column_filter(angular, sign, height, width, core * half, half)
    share(0, shelf)
    for e in range(final - 1, 0, -1):
        pieces[e] = [swap_z(messages[e][0], e)]
    for e in range(1, final):
        share(e)
    book = jnp.swapaxes(speeds[0].reshape(rows, -1, LANES), 0, 1)[None]
    book = jnp.concatenate([book, swap_z(book, top)])
    pieces[final] = []
    for i, message in enumerate(messages[final]):
        ready = (pieces[1], full[0][2]) if i == 0 else (pieces[top], full[1][2], filt)
        pieces[final].append(swap_z(after(message, ready), final))
    for bit in bits(groups)[1:]:
        book = jnp.concatenate([book, swap_z(book, bit)])
    share(final, *([(full[0], full[1][2])] + [(full[1], full[top][2])] * (half // 2 - 1)))
    books = [swap_y(after(book, pieces[final]), r) if r else book for r in range(across)]
    facing = [swap_core(part) for part in books]
    tops = lax.ppermute(after(speeds[1][-1:], pieces[final]), "strip", [(i, i + 1) for i in range(strips - 1)])
    tails = lax.ppermute(after(speeds[1][:1], pieces[final]), "strip", [(i + 1, i) for i in range(strips - 1)])

    scales = jnp.stack([angular, sign])
    books[0], tops, tails = lax.optimization_barrier((books[0], tops, tails))
    beside = jnp.concatenate([jnp.where(me == 0, 1.0, tops), jnp.where(me == strips - 1, 1.0, tails)])

    chosen = [piece for e in range(groups) for lot in full[e] for piece in lot]
    mine, give = enter_columns(ids, chosen, filt, tab, groups, across, rows, half)
    other = swap_core(give)
    factors = prepare(ids, scales, books, facing, groups, across)
    mine, give, near, far = middle(ids, mine, other, factors, tab, groups, across, rows, half)

    other = swap_core(give)
    outs = leave_columns(ids, mine, other, filt, tab, groups, across, rows, half)

    arrived = []
    for e in range(groups):
        kept, given = outs[2 * e], outs[2 * e + 1]
        if e:
            given, kept = swap_z(given, e), swap_z(kept, e)
        arrived += [kept, swap_core(given)]

    facing = swap_z(far, 1)
    facing = after(facing, arrived[2])
    image = near[0] * facing[0] + near[1] * facing[1]

    wide = width // planes

    def spread(value):
        part = lambda k: lax.dynamic_slice_in_dim(value, ((plane + k) % planes) * wide, wide, axis=value.ndim - 1)
        total = part(0)
        for k in range(1, planes):
            total = total + ahead_plane(part(k), k)
        return total

    image = spread(image)
    first_image = lax.dynamic_index_in_dim(image, z // 2, 0, keepdims=False)
    for d in range(1, groups // 2):
        piece = lax.dynamic_index_in_dim(image, (z // 2) ^ d, 0, keepdims=False)
        first_image = first_image + swap_z(piece, 2 * d)

    numbers = jnp.arange(freq_local, dtype=jnp.int32) + plane * freq_local
    angulars = omega_top * (numbers + 1).astype(F32) / freq_total
    source_out, receiver_out, last_image = last(ids, angulars, speeds[1], beside, arrived, tab, groups)
    depth_image = jnp.stack([first_image, spread(last_image)])
    return (depth_image, source_out, receiver_out)


def solution(mesh):
    return jax.shard_map(
        local,
        mesh=mesh,
        in_specs=(
            P(None, "freq", "strip", None),
            P(None, "freq", "strip", None),
            P("freq", "strip", None),
            P(),
        ),
        out_specs=(
            P(None, "strip", "freq"),
            P(None, "freq", "strip", None),
            P(None, "freq", "strip", None),
        ),
        check_vma=False,
    )
```

```python
import functools
import math

import jax
import jax.numpy as jnp
import numpy as np
from jax import lax
from jax.experimental import pallas as pl
from jax.experimental.pallas import tpu as pltpu
from jax.sharding import PartitionSpec as P

DEPTHS = 2

step_length = 0.15
omega_top = 1.2
stencil_gain = 0.05
stencil_damping = 0.1

LANES = 128
ROWS = 16
MIB = 1024 * 1024
ANY = pl.BlockSpec(memory_space=pl.ANY)
VMEM = pl.BlockSpec(memory_space=pltpu.VMEM)
SMEM = pl.BlockSpec(memory_space=pltpu.SMEM)
F32 = jnp.float32
BF16 = jnp.bfloat16


def halves(table):
    table = np.asarray(table, np.float32)
    high = table.astype(jnp.bfloat16)
    low = (table - high.astype(np.float32)).astype(jnp.bfloat16)
    return high, low


def point_tables():
    index = np.arange(LANES)
    angle = 2.0 * np.pi * (index[:, None] * index[None, :] % LANES) / LANES
    cosine, sine = np.cos(angle), np.sin(angle)
    forward = np.block([[cosine, -sine], [sine, cosine]])
    return forward, forward.T


def twiddles(radix):
    length = radix * LANES
    angle = 2.0 * np.pi * (np.arange(radix)[:, None] * np.arange(LANES)[None, :]) / length
    return np.stack([np.cos(angle), -np.sin(angle)]).astype(np.float32)


def small_dft(real, imag, sign):
    count = len(real)
    if count == 1:
        return list(real), list(imag)
    even = small_dft(real[0::2], imag[0::2], sign)
    odd = small_dft(real[1::2], imag[1::2], sign)
    half = count // 2
    top_real, top_imag, low_real, low_imag = [], [], [], []
    for k in range(half):
        o_re, o_im = odd[0][k], odd[1][k]
        if k == 0:
            t_re, t_im = o_re, o_im
        elif 4 * k == count:
            t_re, t_im = (-o_im, o_re) if sign > 0 else (o_im, -o_re)
        elif 8 * k == count:
            h = math.sqrt(0.5)
            t_re, t_im = ((o_re - o_im) * h, (o_im + o_re) * h) if sign > 0 else ((o_re + o_im) * h, (o_im - o_re) * h)
        elif 8 * k == 3 * count:
            h = math.sqrt(0.5)
            t_re, t_im = ((-o_re - o_im) * h, (o_re - o_im) * h) if sign > 0 else ((o_im - o_re) * h, (-o_re - o_im) * h)
        else:
            w_re, w_im = math.cos(2 * math.pi * k / count), sign * math.sin(2 * math.pi * k / count)
            t_re, t_im = o_re * w_re - o_im * w_im, o_re * w_im + o_im * w_re
        top_real.append(even[0][k] + t_re)
        top_imag.append(even[1][k] + t_im)
        low_real.append(even[0][k] - t_re)
        low_imag.append(even[1][k] - t_im)
    return top_real + low_real, top_imag + low_imag


def parts(value):
    high = value.astype(BF16)
    return high, (value - high.astype(F32)).astype(BF16)


def dot(left, right):
    return jnp.dot(left, right, preferred_element_type=F32)


def dot_right(high, low, table):
    return dot(high, table[0]) + dot(low, table[0]) + dot(high, table[1])


def dot_left(both, data_high, data_low):
    size = both.shape[0] // 2
    first = dot(both[...], data_high)
    return first[:size] + first[size:] + dot(both[:size], data_low)


def lanes(k, count=1):
    return slice(k * LANES, (k + count) * LANES)


def turned(re, im, twist, k, row, back):
    if k == 0:
        return re, im
    c, s = twist[0, k, row, :], twist[1, k, row, :]
    if back:
        return re * c + im * s, im * c - re * s
    return re * c - im * s, re * s + im * c


def forward_into(load, row, twist, high, low, index):
    radix = twist.shape[1]
    real, imag = zip(*[load(a) for a in range(radix)])
    real, imag = small_dft(list(real), list(imag), -1)
    for k in range(radix):
        pair = turned(real[k], imag[k], twist, k, slice(0, 1), False)
        for part in (0, 1):
            h, l = parts(pair[part])
            high[index(k) + (row, lanes(part))] = h
            low[index(k) + (row, lanes(part))] = l


def inverse_tiles(load, size, table, twist):
    radix = twist.shape[1]
    data = jnp.concatenate([jnp.concatenate([load(k, 0), load(k, 1)], axis=1) for k in range(radix)], axis=0)
    result = dot_right(*parts(data), table)
    real, imag = [], []
    for k in range(radix):
        row = slice(k * size, (k + 1) * size)
        re, im = turned(result[row, lanes(0)], result[row, lanes(1)], twist, k, slice(0, 1), True)
        real.append(re)
        imag.append(im)
    return small_dft(real, imag, 1)


class Copies:
    def __init__(self, sems):
        self.sems, self.used = sems, 0

    def __call__(self, *pairs):
        made = []
        for source, target in pairs:
            made.append(pltpu.make_async_copy(source, target, self.sems.at[self.used]))
            self.used += 1
        for copy in made:
            copy.start()
        return made


def done(copies):
    for copy in copies:
        copy.wait()


def call(kernel, name, out_shape, in_specs, out_specs, scratch, limit, flops, moved, args):
    return pl.pallas_call(
        kernel,
        out_shape=out_shape,
        in_specs=in_specs,
        out_specs=out_specs,
        scratch_shapes=scratch,
        compiler_params=pltpu.CompilerParams(vmem_limit_bytes=limit * MIB),
        cost_estimate=pl.CostEstimate(flops=flops, bytes_accessed=moved, transcendentals=0),
        name=name,
    )(*args)


def first_kernel(offsets, final, ids, source, receiver, table, twist, *refs):
    high, low, given, out, sems = refs[-5:]
    messages = refs[:-5]
    z, core = ids[0], ids[2]
    radix = twist.shape[1]
    half = radix // 2
    rows = source.shape[2]
    for e, offset in enumerate(offsets):
        field = z ^ offset
        which, number = lax.rem(field, 2), lax.div(field, 2)
        for kind, ref in ((0, source), (1, receiver)):

            @pl.when(which == kind)
            def start(e=e, ref=ref, number=number):
                pltpu.make_async_copy(ref.at[:, number], given.at[e], sems.at[e]).start()

    leaving, used = [], len(offsets)
    place = 0
    for e, offset in enumerate(offsets):
        pltpu.make_async_copy(source.at[:, 0], given.at[e], sems.at[e]).wait()

        def chunk(t, carry, e=e):
            row = pl.ds(pl.multiple_of(t * ROWS, ROWS), ROWS)
            forward_into(
                lambda a: (given[e, 0, row, lanes(a)], given[e, 1, row, lanes(a)]), row, twist, high, low, lambda k: (e, k)
            )
            return carry

        lax.fori_loop(0, rows // ROWS, chunk, 0)
        for slot, start in ((0, core * half), (1, (1 - core) * half)):
            h = high[e, pl.ds(start, half)].reshape(half * rows, 2 * LANES)
            l = low[e, pl.ds(start, half)].reshape(half * rows, 2 * LANES)
            result = dot_right(h, l, table)
            for k in range(half):
                for part in (0, 1):
                    at = (slot * half + k) * 2 + part
                    out[e, at * rows : (at + 1) * rows, :] = result[k * rows : (k + 1) * rows, lanes(part)]
        moves = []
        if offset == final:
            for p in range(half // 2):
                for slot in (0, 1):
                    moves.append(
                        (
                            out.at[e, pl.ds((slot * half + 2 * p) * 2 * rows, 4 * rows)],
                            messages[place].at[pl.ds(slot * 4 * rows, 4 * rows)],
                        )
                    )
                place += 1
        else:
            moves.append((out.at[e], messages[place]))
            place += 1
        for source_part, target in moves:
            copy = pltpu.make_async_copy(source_part, target, sems.at[used])
            copy.start()
            leaving.append(copy)
            used += 1
    done(leaving)


def first_transform(ids, source, receiver, offsets, final, tab):
    rows, width = source.shape[2:]
    radix = width // LANES
    tall = 2 * radix * rows
    shapes = []
    for offset in offsets:
        if offset == final:
            shapes += [jax.ShapeDtypeStruct((8 * rows, LANES), F32)] * (radix // 4)
        else:
            shapes.append(jax.ShapeDtypeStruct((tall, LANES), F32))
    count = len(offsets)
    return call(
        functools.partial(first_kernel, offsets, final),
        "first_transform",
        tuple(shapes),
        [SMEM, ANY, ANY, VMEM, VMEM],
        (ANY,) * len(shapes),
        [
            pltpu.VMEM((count, radix, rows, 2 * LANES), BF16),
            pltpu.VMEM((count, radix, rows, 2 * LANES), BF16),
            pltpu.VMEM((count, 2, rows, width), F32),
            pltpu.VMEM((count, tall, LANES), F32),
            pltpu.SemaphoreType.DMA((count + 2 * len(shapes),)),
        ],
        56,
        count * 1000000000,
        count * 1000000,
        (ids, source, receiver, tab["right_forward"], tab["twist_y"]),
    )


def shift_columns(pairs, ready, leave, rows, data, filt_re, filt_im, ahead, back, twist, high, low, line):
    radix = twist.shape[1]
    per = rows // ROWS

    def spot(k, part, a, t):
        index = a * (LANES // ROWS) + t
        block, inner = index // per, index % per
        start = (2 * k + part) * rows + inner * ROWS
        return block // 2, block % 2, slice(start, start + ROWS)

    def fold(pair, t):
        slot = pair % 2
        off = t * ROWS
        row = slice(off, off + ROWS)
        for kk in (0, 1):
            real, imag = ([data[spot(2 * pair + kk, part, a, t)] for a in range(radix)] for part in (0, 1))
            real, imag = small_dft(real, imag, -1)
            for k in range(radix):
                turn_pair = turned(real[k], imag[k], twist, k, row, False)
                for part in (0, 1):
                    h, l = parts(turn_pair[part])
                    at = slice(part * LANES + off, part * LANES + off + ROWS)
                    high[slot, k, at, lanes(kk)] = h
                    low[slot, k, at, lanes(kk)] = l

    def spectral(pair, k):
        slot = pair % 2
        value = dot_left(ahead, high[slot, k], low[slot, k])
        re, im = value[:LANES], value[LANES:]
        fr = jnp.concatenate([filt_re[2 * pair, k], filt_re[2 * pair + 1, k]], axis=1)
        fi = jnp.concatenate([filt_im[2 * pair, k], filt_im[2 * pair + 1, k]], axis=1)
        both = jnp.concatenate([re * fr - im * fi, re * fi + im * fr], axis=0)
        h, l = parts(both)
        line[slot, k] = dot_left(back, h, l)

    def unfold(pair, t):
        slot = pair % 2
        off = t * ROWS
        row = slice(off, off + ROWS)
        for kk in (0, 1):
            real, imag = [], []
            for k in range(radix):
                re = line[slot, k, off : off + ROWS, lanes(kk)]
                im = line[slot, k, LANES + off : LANES + off + ROWS, lanes(kk)]
                re, im = turned(re, im, twist, k, row, True)
                real.append(re)
                imag.append(im)
            both = small_dft(real, imag, 1)
            for part in (0, 1):
                for a in range(radix):
                    data[spot(2 * pair + kk, part, a, t)] = both[part][a]

    chunks = LANES // ROWS
    ready(0)
    for t in range(chunks):
        fold(0, t)
    for pair in range(pairs):
        if pair + 1 < pairs:
            ready(pair + 1)
        for t in range(max(radix, chunks)):
            if t < radix:
                spectral(pair, t)
            if t < chunks and pair + 1 < pairs:
                fold(pair + 1, t)
            if t < chunks and pair > 0:
                unfold(pair - 1, t)
        if pair > 0:
            leave(pair - 1)
    for t in range(chunks):
        unfold(pairs - 1, t)
    leave(pairs - 1)


def outer_rows(rows, half, data):
    count = data.shape[0]
    for b in range(2 * count):
        for k in range(half):
            for part in (0, 1):
                base = (2 * k + part) * rows
                at = 2 * half * rows + (2 * k + part) * 2
                for side, beside, row in ((0, b - 1, base + rows - 1), (1, b + 1, base)):
                    if 0 <= beside < 2 * count:
                        value = data[beside // 2, beside % 2, row : row + 1, :]
                    else:
                        value = jnp.zeros((1, LANES), F32)
                    data[b // 2, b % 2, at + side : at + side + 1, :] = value


def enter_kernel(groups, across, rows, ids, filt_re, filt_im, ahead, back, twist, *refs):
    keep, send, data, fre, fim, tw, high, low, line, sems = refs[-10:]
    pieces = refs[:-10]
    z, y, core = ids[0], ids[1], ids[2]
    half = fre.shape[0]
    pairs = half // 2
    copies = Copies(sems)
    first = copies((twist, tw))
    arrivals = []
    for p in range(pairs):
        moves = []
        at = 0
        for e in range(groups):
            split = e == groups - 1
            for r in range(across):
                block = (z ^ e) * across + (y ^ r)
                for h in (0, 1):
                    piece = pieces[at + (p if split else 0)]
                    at += pairs if split else 1
                    start = h * 4 * rows if split else (h * half + 2 * p) * 2 * rows
                    moves.append(
                        (
                            piece.at[pl.ds(start, 4 * rows)],
                            data.at[block, core ^ h, pl.ds(4 * p * rows, 4 * rows)],
                        )
                    )
        moves += [(a.at[pl.ds(2 * p, 2)], b.at[pl.ds(2 * p, 2)]) for a, b in ((filt_re, fre), (filt_im, fim))]
        arrivals.append(copies(*moves))
    done(first)
    leaving = []

    def leave(p):
        lot = pl.ds(4 * p * rows, 4 * rows)
        leaving.extend(copies(*[(data.at[:, par, lot], out.at[:, lot]) for out, par in ((send, 1 - core), (keep, core))]))

    ready = lambda p: done(arrivals[p])
    shift_columns(pairs, ready, leave, rows, data, fre, fim, ahead, back, tw, high, low, line)
    outer_rows(rows, half, data)
    lot = pl.ds(2 * half * rows, 4 * half)
    leaving += copies(*[(data.at[:, par, lot], out.at[:, lot]) for out, par in ((send, 1 - core), (keep, core))])
    done(leaving)


def leave_kernel(groups, across, rows, ids, filt_re, filt_im, ahead, back, twist, mine, other, *refs):
    data, fre, fim, tw, high, low, line, sems = refs[-8:]
    outs = refs[:-8]
    z, y, core = ids[0], ids[1], ids[2]
    half = fre.shape[0]
    pairs = half // 2
    copies = Copies(sems)
    first = copies((twist, tw))
    arrivals = []
    for p in range(pairs):
        lot = pl.ds(4 * p * rows, 4 * rows)
        moves = [(mine.at[:, lot], data.at[:, core, lot]), (other.at[:, lot], data.at[:, 1 - core, lot])]
        moves += [(a.at[pl.ds(2 * p, 2)], b.at[pl.ds(2 * p, 2)]) for a, b in ((filt_re, fre), (filt_im, fim))]
        arrivals.append(copies(*moves))
    done(first)
    ready = lambda p: done(arrivals[p])
    shift_columns(pairs, ready, lambda p: None, rows, data, fre, fim, ahead, back, tw, high, low, line)
    outer_rows(rows, half, data)
    moves = []
    for e in range(groups):
        for h in (0, 1):
            moves.append((data.at[(z ^ e) * across + y, core ^ h], outs[e].at[h]))
    done(copies(*moves))


def column_scratch(half, count, rows, copies):
    radix = 2 * count * rows // LANES
    return [
        pltpu.VMEM((count, 2, 2 * half * rows + 4 * half, LANES), F32),
        pltpu.VMEM((half, radix, LANES, LANES), F32),
        pltpu.VMEM((half, radix, LANES, LANES), F32),
        pltpu.VMEM((2, radix, LANES, LANES), F32),
        pltpu.VMEM((2, radix, 2 * LANES, 2 * LANES), BF16),
        pltpu.VMEM((2, radix, 2 * LANES, 2 * LANES), BF16),
        pltpu.VMEM((2, radix, 2 * LANES, 2 * LANES), F32),
        pltpu.SemaphoreType.DMA((copies,)),
    ]


def enter_columns(ids, pieces, filt, tab, groups, across, rows, half):
    count = groups * across
    out = jax.ShapeDtypeStruct((count, 2 * half * rows + 4 * half, LANES), F32)
    pairs = half // 2
    return call(
        functools.partial(enter_kernel, groups, across, rows),
        "enter_columns",
        (out, out),
        [SMEM, ANY, ANY, VMEM, VMEM, ANY] + [ANY] * len(pieces),
        (ANY, ANY),
        column_scratch(half, count, rows, 1 + pairs * (2 * count + 4) + 2),
        56,
        8000000000,
        8000000,
        (ids, *filt, tab["left_forward"], tab["left_inverse"], tab["twist_x"], *pieces),
    )


def leave_columns(ids, mine, other, filt, tab, groups, across, rows, half):
    count = groups * across
    out = jax.ShapeDtypeStruct((2, 2 * half * rows + 4 * half, LANES), F32)
    return call(
        functools.partial(leave_kernel, groups, across, rows),
        "leave_columns",
        (out,) * groups,
        [SMEM, ANY, ANY, VMEM, VMEM, ANY, ANY, ANY],
        (ANY,) * groups,
        column_scratch(half, count, rows, 1 + 2 * half + 2 * groups),
        19,
        8000000000,
        8000000,
        (ids, *filt, tab["left_forward"], tab["left_inverse"], tab["twist_x"], mine, other),
    )


def turn(square):
    cosine = 1.0 + square * (-1.0 / 2 + square * (1.0 / 24 + square * (-1.0 / 720)))
    ratio = 1.0 + square * (-1.0 / 6 + square * (1.0 / 120 + square * (-1.0 / 5040)))
    return cosine, ratio


def correction(speed, angular, sign):
    phase = (sign * step_length) * angular * (1.0 / speed - 1.0)
    cosine, ratio = turn(phase * phase)
    return cosine, ratio * phase, stencil_gain * (speed * speed - 1.0) * angular / omega_top


def stencil(field, halo, weight, sign, store):
    radix, weigh = weight
    shape = field(0, 0).shape
    line = lax.broadcasted_iota(jnp.int32, shape, 0)
    place = lax.broadcasted_iota(jnp.int32, shape, 1)
    top, bottom = line == 0, line == shape[0] - 1
    left, right = place == 0, place == LANES - 1
    zero = jnp.zeros(shape, F32)
    before = [zero, zero]
    for a in range(radix):
        center, bent = [], []
        for part in (0, 1):
            value = field(part, a)
            ahead = pltpu.roll(value, 1, axis=1)
            west = jnp.where(left, before[part], ahead)
            before[part] = ahead
            follow = pltpu.roll(field(part, a + 1), LANES - 1, axis=1) if a + 1 < radix else zero
            east = jnp.where(right, follow, pltpu.roll(value, LANES - 1, axis=1))
            north = jnp.where(top, halo(part, 0, a), pltpu.roll(value, 1, axis=0))
            south = jnp.where(bottom, halo(part, 1, a), pltpu.roll(value, shape[0] - 1, axis=0))
            center.append(value)
            bent.append((north + south) + (west + east) - 4.0 * value)
        heavy = weigh(a)
        twist, damp = heavy * sign, heavy * stencil_damping
        store(0, a, center[0] + damp * bent[0] - twist * bent[1])
        store(1, a, center[1] + damp * bent[1] + twist * bent[0])


def middle_kernel(groups, across, rows, ids, back, ahead, twist, halo_cos, halo_sin, cosine, sine, weight, mine, other, *refs):
    keep, send, near, far, data, halo, cos, sin, wei, field, edge, fresh, high, low, out, block_sems, sems = refs
    z, y, core = ids[0], ids[1], ids[2]
    which = lax.rem(z, 2)
    sign = jnp.where(which == 0, -1.0, 1.0).astype(F32)
    count = groups * across
    radix = twist.shape[1]
    half = radix // 2
    own, outer = pl.ds(0, 2 * half * rows), pl.ds(2 * half * rows, 4 * half)
    copies = Copies(sems)
    first = copies((mine.at[:, outer], halo.at[core]), (other.at[:, outer], halo.at[1 - core]))

    def arrivals(i):
        pairs = (
            (mine.at[i, own], data.at[core, i]),
            (other.at[i, own], data.at[1 - core, i]),
            (cosine.at[i], cos.at[i]),
            (sine.at[i], sin.at[i]),
            (weight.at[i], wei.at[i]),
        )
        return [pltpu.make_async_copy(a, b, block_sems.at[i, n]) for n, (a, b) in enumerate(pairs)]

    def launch(i, carry):
        for copy in arrivals(i):
            copy.start()
        return carry

    lax.fori_loop(0, count, launch, 0)
    done(first)

    def halo_rows(k, part):
        at = (2 * (k % half) + part) * 2
        return jnp.concatenate([halo[k // half, i, at : at + 2, :] for i in range(count)], axis=0)

    real, imag = inverse_tiles(halo_rows, 2 * count, back, twist)
    for a in range(radix):
        c, s = halo_cos[a], halo_sin[a]
        edge[0, a] = real[a] * c - imag[a] * s
        edge[1, a] = real[a] * s + imag[a] * c

    def departures(i):
        pairs = ((out.at[1, i], send.at[i]), (out.at[0, i], keep.at[i]))
        return [pltpu.make_async_copy(a, b, block_sems.at[i, n]) for n, (a, b) in enumerate(pairs)]

    def step(j, carry):
        for b in (0, 1):
            i = 2 * j + b
            done(arrivals(i))
            real, imag = inverse_tiles(
                lambda k, part: data[k // half, i, (2 * (k % half) + part) * rows : (2 * (k % half) + part + 1) * rows, :],
                rows,
                back,
                twist,
            )
            for a in range(radix):
                c, s = cos[i, a], sin[i, a]
                field[b, 0, a] = real[a] * c - imag[a] * s
                field[b, 1, a] = real[a] * s + imag[a] * c
        for b in (0, 1):
            i = 2 * j + b

            def store(part, a, value):
                fresh[part, i, :, lanes(a)] = value

            stencil(
                lambda part, a: field[b, part, a],
                lambda part, side, a: edge[part, a, pl.ds(2 * i + side, 1), :],
                (radix, lambda a: wei[i, a]),
                sign,
                store,
            )
            for t in range(rows // ROWS):
                row = slice(t * ROWS, (t + 1) * ROWS)
                forward_into(
                    lambda a: (fresh[0, i, row, lanes(a)], fresh[1, i, row, lanes(a)]),
                    row,
                    twist,
                    high,
                    low,
                    lambda k: (b, k),
                )
        for b in (0, 1):
            i = 2 * j + b
            for slot, start in ((1, (1 - core) * half), (0, core * half)):
                h = high[b, pl.ds(start, half)].reshape(half * rows, 2 * LANES)
                l = low[b, pl.ds(start, half)].reshape(half * rows, 2 * LANES)
                result = dot_right(h, l, ahead)
                for k in range(half):
                    for part in (0, 1):
                        at = 2 * k + part
                        out[slot, i, at * rows : (at + 1) * rows, :] = result[k * rows : (k + 1) * rows, lanes(part)]
            for copy in departures(i):
                copy.start()
        return carry

    lax.fori_loop(0, count // 2, step, 0)
    leaving = []
    for target, parity in ((far, 1 - which), (near, which)):
        for t in range(groups // 2):
            leaving += copies((fresh.at[:, (parity + 2 * t) * across + y], target.at[:, t]))

    def settle(i, carry):
        done(departures(i))
        return carry

    lax.fori_loop(0, count, settle, 0)
    done(leaving)


def middle(ids, mine, other, factors, tab, groups, across, rows, half):
    count = groups * across
    radix = 2 * half
    width = radix * LANES
    out = jax.ShapeDtypeStruct((count, 2 * half * rows, LANES), F32)
    image = jax.ShapeDtypeStruct((2, groups // 2, rows, width), F32)
    cosine, sine, weight, halo_cos, halo_sin = factors
    blocks = pltpu.VMEM((count, radix, rows, LANES), F32)
    return call(
        functools.partial(middle_kernel, groups, across, rows),
        "middle",
        (out, out, image, image),
        [SMEM] + [VMEM] * 5 + [ANY] * 5,
        (ANY,) * 4,
        [
            pltpu.VMEM((2, count, 2 * half * rows, LANES), F32),
            pltpu.VMEM((2, count, 4 * half, LANES), F32),
            blocks,
            blocks,
            blocks,
            pltpu.VMEM((2, 2, radix, rows, LANES), F32),
            pltpu.VMEM((2, radix, 2 * count, LANES), F32),
            pltpu.VMEM((2, count, rows, width), F32),
            pltpu.VMEM((2, radix, rows, 2 * LANES), BF16),
            pltpu.VMEM((2, radix, rows, 2 * LANES), BF16),
            pltpu.VMEM((2, count, 2 * half * rows, LANES), F32),
            pltpu.SemaphoreType.DMA((count, 5)),
            pltpu.SemaphoreType.DMA((2 + groups,)),
        ],
        23,
        16000000000,
        10000000,
        (
            ids,
            tab["right_inverse"],
            tab["right_forward"],
            tab["twist_y"],
            halo_cos,
            halo_sin,
            cosine,
            sine,
            weight,
            mine,
            other,
        ),
    )


def prepare_kernel(groups, across, lots, ids, scales, *refs):
    number = len(lots)
    pieces, others = refs[:number], refs[number : 2 * number]
    outs, (halo_cos, halo_sin, ends) = refs[2 * number : 2 * number + 3], refs[2 * number + 3 : 2 * number + 6]
    speed, held, lasts, firsts, later, block_sems, sems = refs[2 * number + 6 :]
    z, y, core = ids[0], ids[1], ids[2]
    count, radix, rows, _ = speed.shape
    one = jnp.ones((radix, 8, LANES), F32)
    lasts[0] = one
    firsts[count] = one
    later[0] = one
    later[count] = one
    copies = Copies(sems)
    moves, beside, places = [], [], []
    for piece, other, (offsets, r) in zip(pieces, others, lots):
        for n, e in enumerate(offsets):
            block = (z ^ e) * across + (y ^ r)
            places.append((e, r))
            moves.append((piece.at[n, :, pl.ds(0, rows)], speed.at[len(moves)]))
            beside.append((other.at[n, :, pl.ds(16, 8)], later.at[block + 1 - core]))
            beside.append((other.at[n, :, pl.ds(8, 8)], lasts.at[block + 1 - core]))
            beside.append((other.at[n, :, pl.ds(0, 8)], firsts.at[block + 1 - core]))
    moves, beside = copies(*moves), copies(*beside)
    done(moves)

    def departures(i):
        e = sum(jnp.where(i == at, e, 0) for at, (e, _) in enumerate(places))
        r = sum(jnp.where(i == at, r, 0) for at, (_, r) in enumerate(places))
        block = (z ^ e) * across + (y ^ r)
        return [pltpu.make_async_copy(held.at[m, i], outs[m].at[block], block_sems.at[i, m]) for m in range(3)]

    def chunk(i, carry):
        for a in range(radix):
            held[0, i, a], held[1, i, a], held[2, i, a] = correction(speed[i, a], scales[0], scales[1])
        for copy in departures(i):
            copy.start()
        return carry

    lax.fori_loop(0, count, chunk, 0)
    done(beside)
    for a in range(radix):
        rows_beside = []
        for i in range(count):
            rows_beside += [lasts[i, a, 7:8, :], firsts[i + 1, a, 0:1, :]]
        halo_cos[a], halo_sin[a], _ = correction(jnp.concatenate(rows_beside, axis=0), scales[0], scales[1])
    mine = z * across + y
    for a in range(radix):
        ends[a] = jnp.concatenate([later[mine, a, 1:2, :], later[mine + 1, a, 0:1, :]], axis=0)

    def settle(i, carry):
        done(departures(i))
        return carry

    lax.fori_loop(0, count, settle, 0)


def prepare(ids, scales, books, others, groups, across, rows):
    pieces = [held for held, _, _ in books]
    lots = [(tuple(offsets), r) for _, offsets, r in books]
    radix = pieces[0].shape[1]
    count = groups * across
    out = jax.ShapeDtypeStruct((count, radix, rows, LANES), F32)
    halo = jax.ShapeDtypeStruct((radix, 2 * count, LANES), F32)
    return call(
        functools.partial(prepare_kernel, groups, across, lots),
        "prepare",
        (out, out, out, halo, halo, jax.ShapeDtypeStruct((radix, 2, LANES), F32)),
        [SMEM] * 2 + [ANY] * (2 * len(pieces)),
        (ANY,) * 3 + (VMEM,) * 3,
        [
            pltpu.VMEM((count, radix, rows, LANES), F32),
            pltpu.VMEM((3, count, radix, rows, LANES), F32),
            pltpu.VMEM((count + 1, radix, 8, LANES), F32),
            pltpu.VMEM((count + 1, radix, 8, LANES), F32),
            pltpu.VMEM((count + 1, radix, 8, LANES), F32),
            pltpu.SemaphoreType.DMA((count, 3)),
            pltpu.SemaphoreType.DMA((4 * count,)),
        ],
        11,
        4000000000,
        8000000,
        (ids, scales, *pieces, *others),
    )


def last_kernel(groups, rows, ids, angulars, back, twist, speed, beside, *refs):
    source, receiver, image, data, field, edge, turns, sems = refs[-8:]
    pieces = refs[:-8]
    z, core = ids[0], ids[2]
    radix = twist.shape[1]
    half = radix // 2
    copies = Copies(sems)
    arrivals = copies(
        *[(pieces[2 * e + h].at[h], data.at[z ^ e, core ^ h]) for e in range(groups) for h in (0, 1)]
    )
    done(arrivals)

    def halo_rows(k, part):
        at = 2 * half * rows + (2 * (k % half) + part) * 2
        return jnp.concatenate(
            [data[g, k // half, at : at + 2, :] for g in range(groups)] + [jnp.zeros((tall - 2 * groups, LANES), F32)], axis=0
        )

    tall = -(-2 * groups // ROWS) * ROWS
    real, imag = inverse_tiles(halo_rows, tall, back, twist)
    for a in range(radix):
        for g in range(groups):
            c, s, _ = correction(beside[a], angulars[g // 2], 2.0 * (g % 2) - 1.0)
            pair = slice(2 * g, 2 * g + 2)
            edge[0, a, pair, :] = real[a][pair] * c - imag[a][pair] * s
            edge[1, a, pair, :] = real[a][pair] * s + imag[a][pair] * c
    for number in range(groups // 2):
        for a in range(radix):
            turns[0, a], turns[1, a], turns[2, a] = correction(speed[:, lanes(a)], angulars[number], 1.0)
        for which, out in ((0, source), (1, receiver)):
            sign = 2.0 * which - 1.0
            g = 2 * number + which
            real, imag = inverse_tiles(
                lambda k, part: data[g, k // half, (2 * (k % half) + part) * rows : (2 * (k % half) + part + 1) * rows, :],
                rows,
                back,
                twist,
            )
            for a in range(radix):
                c, s = turns[0, a], turns[1, a] * sign
                field[0, a] = real[a] * c - imag[a] * s
                field[1, a] = real[a] * s + imag[a] * c

            def store(part, a, value):
                out[part, number, :, lanes(a)] = value

            stencil(
                lambda part, a: field[part, a],
                lambda part, side, a: edge[part, a, 2 * g + side : 2 * g + side + 1, :],
                (radix, lambda a: turns[2, a]),
                sign,
                store,
            )
    for a in range(radix):
        total = jnp.zeros((rows, LANES), F32)
        for number in range(groups // 2):
            for part in (0, 1):
                total = total + source[part, number, :, lanes(a)] * receiver[part, number, :, lanes(a)]
        image[:, lanes(a)] = total


def last(ids, angulars, speed, beside, pieces, tab, groups):
    rows, width = speed.shape
    radix = width // LANES
    out = jax.ShapeDtypeStruct((2, groups // 2, rows, width), F32)
    return call(
        functools.partial(last_kernel, groups, rows),
        "last",
        (out, out, jax.ShapeDtypeStruct((rows, width), F32)),
        [SMEM] * 2 + [VMEM] * 4 + [ANY] * (2 * groups),
        (VMEM,) * 3,
        [
            pltpu.VMEM((groups, 2, radix * rows + 2 * radix, LANES), F32),
            pltpu.VMEM((2, radix, rows, LANES), F32),
            pltpu.VMEM((2, radix, 2 * groups, LANES), F32),
            pltpu.VMEM((3, radix, rows, LANES), F32),
            pltpu.SemaphoreType.DMA((2 * groups,)),
        ],
        12,
        8000000000,
        8000000,
        (ids, angulars, tab["right_inverse"], tab["twist_y"], speed, beside, *pieces),
    )


def gather_order(groups):
    order = [0]
    for bit in bits(groups):
        order += [e ^ bit for e in order]
    return order


def after(value, *others):
    return lax.optimization_barrier((value, others))[0]


def bits(count):
    return [1 << n for n in reversed(range(count.bit_length() - 1))]


def centered(position, length):
    shifted = jnp.where(position < length // 2, position, position - length)
    return shifted.astype(F32) * (2.0 * math.pi / length)


def column_filter(angular, sign, height, width, first_block, blocks):
    radix_x, radix_y = height // LANES, width // LANES
    inner = jnp.arange(LANES, dtype=jnp.int32)
    wave_x = centered(jnp.arange(radix_x, dtype=jnp.int32)[:, None] + radix_x * inner[None, :], height)
    wave_y = centered(first_block + jnp.arange(blocks, dtype=jnp.int32)[:, None] + radix_y * inner[None, :], width)
    wave_x = wave_x[None, :, :, None]
    wave_y = wave_y[:, None, None, :]
    argument = angular * angular - (wave_x * wave_x + wave_y * wave_y)
    radius = step_length * jnp.sqrt(jnp.abs(argument))
    travel = argument >= 0.0
    scale = 1.0 / (height * width)
    cosine, ratio = turn(jnp.where(travel, radius * radius, 0.0))
    real = jnp.where(travel, cosine, jnp.exp(-radius)) * scale
    imag = jnp.where(travel, ratio * radius, 0.0) * (sign * scale)
    return real, imag


def local(source_field, receiver_field, velocity, slice_owner):
    freq_local, rows, width = source_field.shape[1:]
    strips = lax.axis_size("strip")
    planes = lax.axis_size("freq")
    height = rows * strips
    groups = 2 * freq_local
    members = strips // groups
    across = members // 2
    radix = width // LANES
    half = radix // 2
    freq_total = freq_local * planes
    me = lax.axis_index("strip")
    plane = lax.axis_index("freq")
    z, y, core = me // members, (me // 2) % across, me % 2
    ids = jnp.stack([z, y, core, plane]).astype(jnp.int32)

    def swap(value, bit):
        return lax.ppermute(value, "strip", [(i, i ^ bit) for i in range(strips)])

    def swap_z(value, e):
        return swap(value, e * members)

    def swap_y(value, r):
        return swap(value, 2 * r)

    def swap_core(value):
        return swap(value, 1)

    def ahead_plane(value, k):
        return lax.ppermute(value, "freq", [(i, (i + k) % planes) for i in range(planes)])

    forward, inverse = point_tables()
    stack = lambda table: jnp.asarray(np.stack(halves(table)))
    both = lambda table: jnp.asarray(np.concatenate(halves(table)))
    tab = {
        "right_forward": stack(forward),
        "right_inverse": stack(inverse),
        "left_forward": both(forward.T),
        "left_inverse": both(inverse.T),
        "twist_y": jnp.asarray(twiddles(radix)[:, :, None, :]),
        "twist_x": jnp.asarray(np.repeat(twiddles(height // LANES)[..., None], LANES, axis=-1)),
    }

    slots = velocity.shape[0]
    shelf = jnp.stack([velocity] + [ahead_plane(velocity, k) for k in range(1, planes)])

    def own_slice(depth):
        number = slice_owner[depth]
        return lax.dynamic_slice(
            shelf,
            ((plane - number // slots) % planes, number % slots, 0, 0),
            (1, 1, rows, width),
        )[0, 0]

    speeds = [own_slice(depth) for depth in range(DEPTHS)]

    final, top = groups - 1, groups // 2
    messages = {}
    order = [top, 0] + [e for e in range(1, final) if e != top] + [final]
    made = list(first_transform(ids, source_field, receiver_field, order, final, tab))
    for e in order:
        messages[e] = [made.pop(0) for _ in range(half // 2 if e == final else 1)]
    pieces, full = {0: messages[0]}, {}

    def share(e, *waits):
        ready = [after(piece, wait) for piece, wait in zip(pieces[e], waits)] if waits else pieces[e]
        mine = [pieces[e]] + [[] for r in range(1, across)]
        for piece in ready:
            sent = [swap_y(after(piece, mine[r][-1:]), r) for r in range(1, across)]
            for r in range(1, across):
                mine[r].append(sent[r - 1])
        full[e] = [lot for own in mine for lot in (own, [swap_core(piece) for piece in own])]

    angular = omega_top * (plane * freq_local + z // 2 + 1).astype(F32) / freq_total
    sign = jnp.where(z % 2 == 0, -1.0, 1.0).astype(F32)
    filt = column_filter(angular, sign, height, width, core * half, half)
    share(0, shelf)
    for e in range(final - 1, 0, -1):
        pieces[e] = [swap_z(messages[e][0], e)]
    for e in range(1, final):
        share(e)
    book = jnp.concatenate([speeds[0], speeds[1][:1], speeds[1][-1:], jnp.zeros((6, width), F32)])
    book = jnp.swapaxes(book.reshape(rows + 8, -1, LANES), 0, 1)[None]
    books = [(book, [0]), (swap_z(book, top), [top])]
    pieces[final] = []
    for i, message in enumerate(messages[final]):
        ready = (pieces[1], full[0][2]) if i == 0 else (pieces[top], full[1][2], filt)
        pieces[final].append(swap_z(after(message, ready), final))
    for bit in bits(groups)[1:]:
        book, offsets = jnp.concatenate([held for held, _ in books]), [e for _, lot in books for e in lot]
        books = [(book, offsets), (swap_z(book, bit), [e ^ bit for e in offsets])]
    share(final, *([(full[0], full[1][2])] + [(full[1], full[top][2])] * (half // 2 - 1)))
    books = [(held, lot, 0) for held, lot in books] + [
        (swap_y(held if n == 0 else after(held, pieces[final]), r), lot, r)
        for n, (held, lot) in enumerate(books)
        for r in range(1, across)
    ]
    edges = lambda held: jnp.concatenate([held[:, :, :8], held[:, :, rows - 8 :]], axis=2)
    facing = [swap_core(edges(held)) for held, _, _ in books]
    scales = jnp.stack([angular, sign])
    chosen = [piece for e in range(groups) for lot in full[e] for piece in lot]
    mine, give = enter_columns(ids, chosen, filt, tab, groups, across, rows, half)
    other = swap_core(give)
    *factors, beside = prepare(ids, scales, books, facing, groups, across, rows)
    mine, give, near, far = middle(ids, mine, other, factors, tab, groups, across, rows, half)

    other = swap_core(give)
    outs = leave_columns(ids, mine, other, filt, tab, groups, across, rows, half)

    arrived = []
    for e in range(groups):
        piece = swap_z(outs[e], e) if e else outs[e]
        arrived += [piece, swap_core(piece)]

    facing = swap_z(far, 1)
    facing = after(facing, arrived[2])
    image = near[0] * facing[0] + near[1] * facing[1]

    wide = width // planes

    def spread(value):
        part = lambda k: lax.dynamic_slice_in_dim(value, ((plane + k) % planes) * wide, wide, axis=value.ndim - 1)
        total = part(0)
        for k in range(1, planes):
            total = total + ahead_plane(part(k), k)
        return total

    image = spread(image)
    first_image = lax.dynamic_index_in_dim(image, z // 2, 0, keepdims=False)
    for d in range(1, groups // 2):
        piece = lax.dynamic_index_in_dim(image, (z // 2) ^ d, 0, keepdims=False)
        first_image = first_image + swap_z(piece, 2 * d)

    numbers = jnp.arange(freq_local, dtype=jnp.int32) + plane * freq_local
    angulars = omega_top * (numbers + 1).astype(F32) / freq_total
    source_out, receiver_out, last_image = last(ids, angulars, speeds[1], beside, arrived, tab, groups)
    depth_image = jnp.stack([first_image, spread(last_image)])
    return (depth_image, source_out, receiver_out)


def solution(mesh):
    return jax.shard_map(
        local,
        mesh=mesh,
        in_specs=(
            P(None, "freq", "strip", None),
            P(None, "freq", "strip", None),
            P("freq", "strip", None),
            P(),
        ),
        out_specs=(
            P(None, "strip", "freq"),
            P(None, "freq", "strip", None),
            P(None, "freq", "strip", None),
        ),
        check_vma=False,
    )
```

```python
import functools
import math

import jax
import jax.numpy as jnp
import numpy as np
from jax import lax
from jax.experimental import pallas as pl
from jax.experimental.pallas import tpu as pltpu
from jax.sharding import PartitionSpec as P

DEPTHS = 2

step_length = 0.15
omega_top = 1.2
stencil_gain = 0.05
stencil_damping = 0.1

LANES = 128
ROWS = 16
MIB = 1024 * 1024
ANY = pl.BlockSpec(memory_space=pl.ANY)
VMEM = pl.BlockSpec(memory_space=pltpu.VMEM)
SMEM = pl.BlockSpec(memory_space=pltpu.SMEM)
F32 = jnp.float32
BF16 = jnp.bfloat16


def halves(table):
    table = np.asarray(table, np.float32)
    high = table.astype(jnp.bfloat16)
    low = (table - high.astype(np.float32)).astype(jnp.bfloat16)
    return high, low


def point_tables():
    index = np.arange(LANES)
    angle = 2.0 * np.pi * (index[:, None] * index[None, :] % LANES) / LANES
    cosine, sine = np.cos(angle), np.sin(angle)
    forward = np.block([[cosine, -sine], [sine, cosine]])
    return forward, forward.T


def twiddles(radix):
    length = radix * LANES
    angle = 2.0 * np.pi * (np.arange(radix)[:, None] * np.arange(LANES)[None, :]) / length
    return np.stack([np.cos(angle), -np.sin(angle)]).astype(np.float32)


def small_dft(real, imag, sign):
    count = len(real)
    if count == 1:
        return list(real), list(imag)
    even = small_dft(real[0::2], imag[0::2], sign)
    odd = small_dft(real[1::2], imag[1::2], sign)
    half = count // 2
    top_real, top_imag, low_real, low_imag = [], [], [], []
    for k in range(half):
        o_re, o_im = odd[0][k], odd[1][k]
        if k == 0:
            t_re, t_im = o_re, o_im
        elif 4 * k == count:
            t_re, t_im = (-o_im, o_re) if sign > 0 else (o_im, -o_re)
        elif 8 * k == count:
            h = math.sqrt(0.5)
            t_re, t_im = ((o_re - o_im) * h, (o_im + o_re) * h) if sign > 0 else ((o_re + o_im) * h, (o_im - o_re) * h)
        elif 8 * k == 3 * count:
            h = math.sqrt(0.5)
            t_re, t_im = ((-o_re - o_im) * h, (o_re - o_im) * h) if sign > 0 else ((o_im - o_re) * h, (-o_re - o_im) * h)
        else:
            w_re, w_im = math.cos(2 * math.pi * k / count), sign * math.sin(2 * math.pi * k / count)
            t_re, t_im = o_re * w_re - o_im * w_im, o_re * w_im + o_im * w_re
        top_real.append(even[0][k] + t_re)
        top_imag.append(even[1][k] + t_im)
        low_real.append(even[0][k] - t_re)
        low_imag.append(even[1][k] - t_im)
    return top_real + low_real, top_imag + low_imag


def parts(value):
    high = value.astype(BF16)
    return high, (value - high.astype(F32)).astype(BF16)


def dot(left, right):
    return jnp.dot(left, right, preferred_element_type=F32)


def dot_right(high, low, table):
    return dot(high, table[0]) + dot(low, table[0]) + dot(high, table[1])


def dot_left(both, data_high, data_low):
    size = both.shape[0] // 2
    first = dot(both[...], data_high)
    return first[:size] + first[size:] + dot(both[:size], data_low)


def lanes(k, count=1):
    return slice(k * LANES, (k + count) * LANES)


def turned(re, im, twist, k, row, back):
    if k == 0:
        return re, im
    c, s = twist[0, k, row, :], twist[1, k, row, :]
    if back:
        return re * c + im * s, im * c - re * s
    return re * c - im * s, re * s + im * c


def forward_into(load, row, twist, high, low, index):
    radix = twist.shape[1]
    real, imag = zip(*[load(a) for a in range(radix)])
    real, imag = small_dft(list(real), list(imag), -1)
    for k in range(radix):
        pair = turned(real[k], imag[k], twist, k, slice(0, 1), False)
        for part in (0, 1):
            h, l = parts(pair[part])
            high[index(k) + (row, lanes(part))] = h
            low[index(k) + (row, lanes(part))] = l


def inverse_tiles(load, size, table, twist):
    radix = twist.shape[1]
    data = jnp.concatenate([jnp.concatenate([load(k, 0), load(k, 1)], axis=1) for k in range(radix)], axis=0)
    result = dot_right(*parts(data), table)
    real, imag = [], []
    for k in range(radix):
        row = slice(k * size, (k + 1) * size)
        re, im = turned(result[row, lanes(0)], result[row, lanes(1)], twist, k, slice(0, 1), True)
        real.append(re)
        imag.append(im)
    return small_dft(real, imag, 1)


class Copies:
    def __init__(self, sems):
        self.sems, self.used = sems, 0

    def __call__(self, *pairs):
        made = []
        for source, target in pairs:
            made.append(pltpu.make_async_copy(source, target, self.sems.at[self.used]))
            self.used += 1
        for copy in made:
            copy.start()
        return made


def done(copies):
    for copy in copies:
        copy.wait()


def call(kernel, name, out_shape, in_specs, out_specs, scratch, limit, flops, moved, args):
    return pl.pallas_call(
        kernel,
        out_shape=out_shape,
        in_specs=in_specs,
        out_specs=out_specs,
        scratch_shapes=scratch,
        compiler_params=pltpu.CompilerParams(vmem_limit_bytes=limit * MIB),
        cost_estimate=pl.CostEstimate(flops=flops, bytes_accessed=moved, transcendentals=0),
        name=name,
    )(*args)


def first_kernel(offsets, final, ids, source, receiver, table, twist, *refs):
    high, low, given, out, sems = refs[-5:]
    messages = refs[:-5]
    z, core = ids[0], ids[2]
    radix = twist.shape[1]
    half = radix // 2
    rows = source.shape[2]
    for e, offset in enumerate(offsets):
        field = z ^ offset
        which, number = lax.rem(field, 2), lax.div(field, 2)
        for kind, ref in ((0, source), (1, receiver)):

            @pl.when(which == kind)
            def start(e=e, ref=ref, number=number):
                pltpu.make_async_copy(ref.at[:, number], given.at[e], sems.at[e]).start()

    leaving, used = [], len(offsets)
    place = 0
    for e, offset in enumerate(offsets):
        pltpu.make_async_copy(source.at[:, 0], given.at[e], sems.at[e]).wait()

        def chunk(t, carry, e=e):
            row = pl.ds(pl.multiple_of(t * ROWS, ROWS), ROWS)
            forward_into(
                lambda a: (given[e, 0, row, lanes(a)], given[e, 1, row, lanes(a)]), row, twist, high, low, lambda k: (e, k)
            )
            return carry

        lax.fori_loop(0, rows // ROWS, chunk, 0, unroll=True)
        for slot, start in ((0, core * half), (1, (1 - core) * half)):
            h = high[e, pl.ds(start, half)].reshape(half * rows, 2 * LANES)
            l = low[e, pl.ds(start, half)].reshape(half * rows, 2 * LANES)
            result = dot_right(h, l, table)
            for k in range(half):
                for part in (0, 1):
                    at = (slot * half + k) * 2 + part
                    out[e, at * rows : (at + 1) * rows, :] = result[k * rows : (k + 1) * rows, lanes(part)]
        moves = []
        if offset == final:
            for p in range(half // 2):
                for slot in (0, 1):
                    moves.append(
                        (
                            out.at[e, pl.ds((slot * half + 2 * p) * 2 * rows, 4 * rows)],
                            messages[place].at[pl.ds(slot * 4 * rows, 4 * rows)],
                        )
                    )
                place += 1
        else:
            moves.append((out.at[e], messages[place]))
            place += 1
        for source_part, target in moves:
            copy = pltpu.make_async_copy(source_part, target, sems.at[used])
            copy.start()
            leaving.append(copy)
            used += 1
    done(leaving)


def first_transform(ids, source, receiver, offsets, final, tab):
    rows, width = source.shape[2:]
    radix = width // LANES
    tall = 2 * radix * rows
    shapes = []
    for offset in offsets:
        if offset == final:
            shapes += [jax.ShapeDtypeStruct((8 * rows, LANES), F32)] * (radix // 4)
        else:
            shapes.append(jax.ShapeDtypeStruct((tall, LANES), F32))
    count = len(offsets)
    return call(
        functools.partial(first_kernel, offsets, final),
        "first_transform",
        tuple(shapes),
        [SMEM, ANY, ANY, VMEM, VMEM],
        (ANY,) * len(shapes),
        [
            pltpu.VMEM((count, radix, rows, 2 * LANES), BF16),
            pltpu.VMEM((count, radix, rows, 2 * LANES), BF16),
            pltpu.VMEM((count, 2, rows, width), F32),
            pltpu.VMEM((count, tall, LANES), F32),
            pltpu.SemaphoreType.DMA((count + 2 * len(shapes),)),
        ],
        56,
        count * 1000000000,
        count * 1000000,
        (ids, source, receiver, tab["right_forward"], tab["twist_y"]),
    )


def shift_columns(pairs, ready, leave, rows, data, filt_re, filt_im, ahead, back, twist, high, low, line):
    radix = twist.shape[1]
    per = rows // ROWS

    def spot(k, part, a, t):
        index = a * (LANES // ROWS) + t
        block, inner = index // per, index % per
        start = (2 * k + part) * rows + inner * ROWS
        return block // 2, block % 2, slice(start, start + ROWS)

    def fold(pair, t):
        slot = pair % 2
        off = t * ROWS
        row = slice(off, off + ROWS)
        for kk in (0, 1):
            real, imag = ([data[spot(2 * pair + kk, part, a, t)] for a in range(radix)] for part in (0, 1))
            real, imag = small_dft(real, imag, -1)
            for k in range(radix):
                turn_pair = turned(real[k], imag[k], twist, k, row, False)
                for part in (0, 1):
                    h, l = parts(turn_pair[part])
                    at = slice(part * LANES + off, part * LANES + off + ROWS)
                    high[slot, k, at, lanes(kk)] = h
                    low[slot, k, at, lanes(kk)] = l

    def spectral(pair, k):
        slot = pair % 2
        value = dot_left(ahead, high[slot, k], low[slot, k])
        re, im = value[:LANES], value[LANES:]
        fr = jnp.concatenate([filt_re[2 * pair, k], filt_re[2 * pair + 1, k]], axis=1)
        fi = jnp.concatenate([filt_im[2 * pair, k], filt_im[2 * pair + 1, k]], axis=1)
        both = jnp.concatenate([re * fr - im * fi, re * fi + im * fr], axis=0)
        h, l = parts(both)
        line[slot, k] = dot_left(back, h, l)

    def unfold(pair, t):
        slot = pair % 2
        off = t * ROWS
        row = slice(off, off + ROWS)
        for kk in (0, 1):
            real, imag = [], []
            for k in range(radix):
                re = line[slot, k, off : off + ROWS, lanes(kk)]
                im = line[slot, k, LANES + off : LANES + off + ROWS, lanes(kk)]
                re, im = turned(re, im, twist, k, row, True)
                real.append(re)
                imag.append(im)
            both = small_dft(real, imag, 1)
            for part in (0, 1):
                for a in range(radix):
                    data[spot(2 * pair + kk, part, a, t)] = both[part][a]

    chunks = LANES // ROWS
    ready(0)
    for t in range(chunks):
        fold(0, t)
    for pair in range(pairs):
        if pair + 1 < pairs:
            ready(pair + 1)
        for t in range(max(radix, chunks)):
            if t < radix:
                spectral(pair, t)
            if t < chunks and pair + 1 < pairs:
                fold(pair + 1, t)
            if t < chunks and pair > 0:
                unfold(pair - 1, t)
        if pair > 0:
            leave(pair - 1)
    for t in range(chunks):
        unfold(pairs - 1, t)
    leave(pairs - 1)


def outer_rows(rows, half, data):
    count = data.shape[0]
    for b in range(2 * count):
        for k in range(half):
            for part in (0, 1):
                base = (2 * k + part) * rows
                at = 2 * half * rows + (2 * k + part) * 2
                for side, beside, row in ((0, b - 1, base + rows - 1), (1, b + 1, base)):
                    if 0 <= beside < 2 * count:
                        value = data[beside // 2, beside % 2, row : row + 1, :]
                    else:
                        value = jnp.zeros((1, LANES), F32)
                    data[b // 2, b % 2, at + side : at + side + 1, :] = value


def enter_kernel(groups, across, rows, ids, filt_re, filt_im, ahead, back, twist, *refs):
    keep, send, data, fre, fim, tw, high, low, line, sems = refs[-10:]
    pieces = refs[:-10]
    z, y, core = ids[0], ids[1], ids[2]
    half = fre.shape[0]
    pairs = half // 2
    copies = Copies(sems)
    first = copies((twist, tw))
    arrivals = []
    for p in range(pairs):
        moves = []
        at = 0
        for e in range(groups):
            split = e == groups - 1
            for r in range(across):
                block = (z ^ e) * across + (y ^ r)
                for h in (0, 1):
                    piece = pieces[at + (p if split else 0)]
                    at += pairs if split else 1
                    start = h * 4 * rows if split else (h * half + 2 * p) * 2 * rows
                    moves.append(
                        (
                            piece.at[pl.ds(start, 4 * rows)],
                            data.at[block, core ^ h, pl.ds(4 * p * rows, 4 * rows)],
                        )
                    )
        moves += [(a.at[pl.ds(2 * p, 2)], b.at[pl.ds(2 * p, 2)]) for a, b in ((filt_re, fre), (filt_im, fim))]
        arrivals.append(copies(*moves))
    done(first)
    leaving = []

    def leave(p):
        lot = pl.ds(4 * p * rows, 4 * rows)
        leaving.extend(copies(*[(data.at[:, par, lot], out.at[:, lot]) for out, par in ((send, 1 - core), (keep, core))]))

    ready = lambda p: done(arrivals[p])
    shift_columns(pairs, ready, leave, rows, data, fre, fim, ahead, back, tw, high, low, line)
    outer_rows(rows, half, data)
    lot = pl.ds(2 * half * rows, 4 * half)
    leaving += copies(*[(data.at[:, par, lot], out.at[:, lot]) for out, par in ((send, 1 - core), (keep, core))])
    done(leaving)


def leave_kernel(groups, across, rows, ids, filt_re, filt_im, ahead, back, twist, mine, other, *refs):
    data, fre, fim, tw, high, low, line, sems = refs[-8:]
    outs = refs[:-8]
    z, y, core = ids[0], ids[1], ids[2]
    half = fre.shape[0]
    pairs = half // 2
    copies = Copies(sems)
    first = copies((twist, tw))
    arrivals = []
    for p in range(pairs):
        lot = pl.ds(4 * p * rows, 4 * rows)
        moves = [(mine.at[:, lot], data.at[:, core, lot]), (other.at[:, lot], data.at[:, 1 - core, lot])]
        moves += [(a.at[pl.ds(2 * p, 2)], b.at[pl.ds(2 * p, 2)]) for a, b in ((filt_re, fre), (filt_im, fim))]
        arrivals.append(copies(*moves))
    done(first)
    ready = lambda p: done(arrivals[p])
    shift_columns(pairs, ready, lambda p: None, rows, data, fre, fim, ahead, back, tw, high, low, line)
    outer_rows(rows, half, data)
    moves = []
    for e in range(groups):
        for h in (0, 1):
            moves.append((data.at[(z ^ e) * across + y, core ^ h], outs[e].at[h]))
    done(copies(*moves))


def column_scratch(half, count, rows, copies):
    radix = 2 * count * rows // LANES
    return [
        pltpu.VMEM((count, 2, 2 * half * rows + 4 * half, LANES), F32),
        pltpu.VMEM((half, radix, LANES, LANES), F32),
        pltpu.VMEM((half, radix, LANES, LANES), F32),
        pltpu.VMEM((2, radix, LANES, LANES), F32),
        pltpu.VMEM((2, radix, 2 * LANES, 2 * LANES), BF16),
        pltpu.VMEM((2, radix, 2 * LANES, 2 * LANES), BF16),
        pltpu.VMEM((2, radix, 2 * LANES, 2 * LANES), F32),
        pltpu.SemaphoreType.DMA((copies,)),
    ]


def enter_columns(ids, pieces, filt, tab, groups, across, rows, half):
    count = groups * across
    out = jax.ShapeDtypeStruct((count, 2 * half * rows + 4 * half, LANES), F32)
    pairs = half // 2
    return call(
        functools.partial(enter_kernel, groups, across, rows),
        "enter_columns",
        (out, out),
        [SMEM, ANY, ANY, VMEM, VMEM, ANY] + [ANY] * len(pieces),
        (ANY, ANY),
        column_scratch(half, count, rows, 1 + pairs * (2 * count + 4) + 2),
        56,
        8000000000,
        8000000,
        (ids, *filt, tab["left_forward"], tab["left_inverse"], tab["twist_x"], *pieces),
    )


def leave_columns(ids, mine, other, filt, tab, groups, across, rows, half):
    count = groups * across
    out = jax.ShapeDtypeStruct((2, 2 * half * rows + 4 * half, LANES), F32)
    return call(
        functools.partial(leave_kernel, groups, across, rows),
        "leave_columns",
        (out,) * groups,
        [SMEM, ANY, ANY, VMEM, VMEM, ANY, ANY, ANY],
        (ANY,) * groups,
        column_scratch(half, count, rows, 1 + 2 * half + 2 * groups),
        19,
        8000000000,
        8000000,
        (ids, *filt, tab["left_forward"], tab["left_inverse"], tab["twist_x"], mine, other),
    )


def turn(square):
    cosine = 1.0 + square * (-1.0 / 2 + square * (1.0 / 24 + square * (-1.0 / 720)))
    ratio = 1.0 + square * (-1.0 / 6 + square * (1.0 / 120 + square * (-1.0 / 5040)))
    return cosine, ratio


def correction(speed, angular, sign):
    phase = (sign * step_length) * angular * (1.0 / speed - 1.0)
    cosine, ratio = turn(phase * phase)
    return cosine, ratio * phase, stencil_gain * (speed * speed - 1.0) * angular / omega_top


def stencil(field, halo, weight, sign, store):
    radix, weigh = weight
    shape = field(0, 0).shape
    line = lax.broadcasted_iota(jnp.int32, shape, 0)
    place = lax.broadcasted_iota(jnp.int32, shape, 1)
    top, bottom = line == 0, line == shape[0] - 1
    left, right = place == 0, place == LANES - 1
    zero = jnp.zeros(shape, F32)
    before = [zero, zero]
    for a in range(radix):
        center, bent = [], []
        for part in (0, 1):
            value = field(part, a)
            ahead = pltpu.roll(value, 1, axis=1)
            west = jnp.where(left, before[part], ahead)
            before[part] = ahead
            follow = pltpu.roll(field(part, a + 1), LANES - 1, axis=1) if a + 1 < radix else zero
            east = jnp.where(right, follow, pltpu.roll(value, LANES - 1, axis=1))
            north = jnp.where(top, halo(part, 0, a), pltpu.roll(value, 1, axis=0))
            south = jnp.where(bottom, halo(part, 1, a), pltpu.roll(value, shape[0] - 1, axis=0))
            center.append(value)
            bent.append((north + south) + (west + east) - 4.0 * value)
        heavy = weigh(a)
        twist, damp = heavy * sign, heavy * stencil_damping
        store(0, a, center[0] + damp * bent[0] - twist * bent[1])
        store(1, a, center[1] + damp * bent[1] + twist * bent[0])


def middle_kernel(groups, across, rows, ids, back, ahead, twist, halo_cos, halo_sin, cosine, sine, weight, mine, other, *refs):
    keep, send, near, far, data, halo, cos, sin, wei, field, edge, fresh, high, low, out, block_sems, sems = refs
    z, y, core = ids[0], ids[1], ids[2]
    which = lax.rem(z, 2)
    sign = jnp.where(which == 0, -1.0, 1.0).astype(F32)
    count = groups * across
    radix = twist.shape[1]
    half = radix // 2
    own, outer = pl.ds(0, 2 * half * rows), pl.ds(2 * half * rows, 4 * half)
    copies = Copies(sems)
    first = copies((mine.at[:, outer], halo.at[core]), (other.at[:, outer], halo.at[1 - core]))

    def arrivals(i):
        pairs = (
            (mine.at[i, own], data.at[core, i]),
            (other.at[i, own], data.at[1 - core, i]),
            (cosine.at[i], cos.at[i]),
            (sine.at[i], sin.at[i]),
            (weight.at[i], wei.at[i]),
        )
        return [pltpu.make_async_copy(a, b, block_sems.at[i, n]) for n, (a, b) in enumerate(pairs)]

    def launch(i, carry):
        for copy in arrivals(i):
            copy.start()
        return carry

    lax.fori_loop(0, count, launch, 0)
    done(first)

    def halo_rows(k, part):
        at = (2 * (k % half) + part) * 2
        return jnp.concatenate([halo[k // half, i, at : at + 2, :] for i in range(count)], axis=0)

    real, imag = inverse_tiles(halo_rows, 2 * count, back, twist)
    for a in range(radix):
        c, s = halo_cos[a], halo_sin[a]
        edge[0, a] = real[a] * c - imag[a] * s
        edge[1, a] = real[a] * s + imag[a] * c

    def departures(i):
        pairs = ((out.at[1, i], send.at[i]), (out.at[0, i], keep.at[i]))
        return [pltpu.make_async_copy(a, b, block_sems.at[i, n]) for n, (a, b) in enumerate(pairs)]

    def step(j, carry):
        for b in (0, 1):
            i = 2 * j + b
            done(arrivals(i))
            real, imag = inverse_tiles(
                lambda k, part: data[k // half, i, (2 * (k % half) + part) * rows : (2 * (k % half) + part + 1) * rows, :],
                rows,
                back,
                twist,
            )
            for a in range(radix):
                c, s = cos[i, a], sin[i, a]
                field[b, 0, a] = real[a] * c - imag[a] * s
                field[b, 1, a] = real[a] * s + imag[a] * c
        for b in (0, 1):
            i = 2 * j + b

            def store(part, a, value):
                fresh[part, i, :, lanes(a)] = value

            stencil(
                lambda part, a: field[b, part, a],
                lambda part, side, a: edge[part, a, pl.ds(2 * i + side, 1), :],
                (radix, lambda a: wei[i, a]),
                sign,
                store,
            )
            for t in range(rows // ROWS):
                row = slice(t * ROWS, (t + 1) * ROWS)
                forward_into(
                    lambda a: (fresh[0, i, row, lanes(a)], fresh[1, i, row, lanes(a)]),
                    row,
                    twist,
                    high,
                    low,
                    lambda k: (b, k),
                )
        for b in (0, 1):
            i = 2 * j + b
            for slot, start in ((1, (1 - core) * half), (0, core * half)):
                h = high[b, pl.ds(start, half)].reshape(half * rows, 2 * LANES)
                l = low[b, pl.ds(start, half)].reshape(half * rows, 2 * LANES)
                result = dot_right(h, l, ahead)
                for k in range(half):
                    for part in (0, 1):
                        at = 2 * k + part
                        out[slot, i, at * rows : (at + 1) * rows, :] = result[k * rows : (k + 1) * rows, lanes(part)]
            for copy in departures(i):
                copy.start()
        return carry

    lax.fori_loop(0, count // 2, step, 0)
    leaving = []
    for target, parity in ((far, 1 - which), (near, which)):
        for t in range(groups // 2):
            leaving += copies((fresh.at[:, (parity + 2 * t) * across + y], target.at[:, t]))

    def settle(i, carry):
        done(departures(i))
        return carry

    lax.fori_loop(0, count, settle, 0)
    done(leaving)


def middle(ids, mine, other, factors, tab, groups, across, rows, half):
    count = groups * across
    radix = 2 * half
    width = radix * LANES
    out = jax.ShapeDtypeStruct((count, 2 * half * rows, LANES), F32)
    image = jax.ShapeDtypeStruct((2, groups // 2, rows, width), F32)
    cosine, sine, weight, halo_cos, halo_sin = factors
    blocks = pltpu.VMEM((count, radix, rows, LANES), F32)
    return call(
        functools.partial(middle_kernel, groups, across, rows),
        "middle",
        (out, out, image, image),
        [SMEM] + [VMEM] * 5 + [ANY] * 5,
        (ANY,) * 4,
        [
            pltpu.VMEM((2, count, 2 * half * rows, LANES), F32),
            pltpu.VMEM((2, count, 4 * half, LANES), F32),
            blocks,
            blocks,
            blocks,
            pltpu.VMEM((2, 2, radix, rows, LANES), F32),
            pltpu.VMEM((2, radix, 2 * count, LANES), F32),
            pltpu.VMEM((2, count, rows, width), F32),
            pltpu.VMEM((2, radix, rows, 2 * LANES), BF16),
            pltpu.VMEM((2, radix, rows, 2 * LANES), BF16),
            pltpu.VMEM((2, count, 2 * half * rows, LANES), F32),
            pltpu.SemaphoreType.DMA((count, 5)),
            pltpu.SemaphoreType.DMA((2 + groups,)),
        ],
        23,
        16000000000,
        10000000,
        (
            ids,
            tab["right_inverse"],
            tab["right_forward"],
            tab["twist_y"],
            halo_cos,
            halo_sin,
            cosine,
            sine,
            weight,
            mine,
            other,
        ),
    )


def prepare_kernel(groups, across, lots, ids, scales, *refs):
    number = len(lots)
    pieces, others = refs[:number], refs[number : 2 * number]
    outs, (halo_cos, halo_sin, ends) = refs[2 * number : 2 * number + 3], refs[2 * number + 3 : 2 * number + 6]
    speed, held, lasts, firsts, later, block_sems, sems = refs[2 * number + 6 :]
    z, y, core = ids[0], ids[1], ids[2]
    count, radix, rows, _ = speed.shape
    one = jnp.ones((radix, 8, LANES), F32)
    lasts[0] = one
    firsts[count] = one
    later[0] = one
    later[count] = one
    copies = Copies(sems)
    moves, beside, places = [], [], []
    for piece, other, (offsets, r) in zip(pieces, others, lots):
        for n, e in enumerate(offsets):
            block = (z ^ e) * across + (y ^ r)
            places.append((e, r))
            moves.append((piece.at[n, :, pl.ds(0, rows)], speed.at[len(moves)]))
            beside.append((other.at[n, :, pl.ds(16, 8)], later.at[block + 1 - core]))
            beside.append((other.at[n, :, pl.ds(8, 8)], lasts.at[block + 1 - core]))
            beside.append((other.at[n, :, pl.ds(0, 8)], firsts.at[block + 1 - core]))
    moves, beside = copies(*moves), copies(*beside)
    done(moves)

    def departures(i):
        e = sum(jnp.where(i == at, e, 0) for at, (e, _) in enumerate(places))
        r = sum(jnp.where(i == at, r, 0) for at, (_, r) in enumerate(places))
        block = (z ^ e) * across + (y ^ r)
        return [pltpu.make_async_copy(held.at[m, i], outs[m].at[block], block_sems.at[i, m]) for m in range(3)]

    def chunk(i, carry):
        for a in range(radix):
            held[0, i, a], held[1, i, a], held[2, i, a] = correction(speed[i, a], scales[0], scales[1])
        for copy in departures(i):
            copy.start()
        return carry

    lax.fori_loop(0, count, chunk, 0)
    done(beside)
    for a in range(radix):
        rows_beside = []
        for i in range(count):
            rows_beside += [lasts[i, a, 7:8, :], firsts[i + 1, a, 0:1, :]]
        halo_cos[a], halo_sin[a], _ = correction(jnp.concatenate(rows_beside, axis=0), scales[0], scales[1])
    mine = z * across + y
    for a in range(radix):
        ends[a] = jnp.concatenate([later[mine, a, 1:2, :], later[mine + 1, a, 0:1, :]], axis=0)

    def settle(i, carry):
        done(departures(i))
        return carry

    lax.fori_loop(0, count, settle, 0)


def prepare(ids, scales, books, others, groups, across, rows):
    pieces = [held for held, _, _ in books]
    lots = [(tuple(offsets), r) for _, offsets, r in books]
    radix = pieces[0].shape[1]
    count = groups * across
    out = jax.ShapeDtypeStruct((count, radix, rows, LANES), F32)
    halo = jax.ShapeDtypeStruct((radix, 2 * count, LANES), F32)
    return call(
        functools.partial(prepare_kernel, groups, across, lots),
        "prepare",
        (out, out, out, halo, halo, jax.ShapeDtypeStruct((radix, 2, LANES), F32)),
        [SMEM] * 2 + [ANY] * (2 * len(pieces)),
        (ANY,) * 3 + (VMEM,) * 3,
        [
            pltpu.VMEM((count, radix, rows, LANES), F32),
            pltpu.VMEM((3, count, radix, rows, LANES), F32),
            pltpu.VMEM((count + 1, radix, 8, LANES), F32),
            pltpu.VMEM((count + 1, radix, 8, LANES), F32),
            pltpu.VMEM((count + 1, radix, 8, LANES), F32),
            pltpu.SemaphoreType.DMA((count, 3)),
            pltpu.SemaphoreType.DMA((4 * count,)),
        ],
        11,
        4000000000,
        8000000,
        (ids, scales, *pieces, *others),
    )


def last_kernel(groups, rows, ids, angulars, back, twist, speed, beside, *refs):
    source_out, receiver_out, image, source, receiver, data, field, edge, turns, sems = refs[-10:]
    pieces = refs[:-10]
    z, core = ids[0], ids[2]
    radix = twist.shape[1]
    half = radix // 2
    copies = Copies(sems)
    arrivals = copies(
        *[(pieces[2 * e + h].at[h], data.at[z ^ e, core ^ h]) for e in range(groups) for h in (0, 1)]
    )
    done(arrivals)

    def halo_rows(k, part):
        at = 2 * half * rows + (2 * (k % half) + part) * 2
        return jnp.concatenate(
            [data[g, k // half, at : at + 2, :] for g in range(groups)] + [jnp.zeros((tall - 2 * groups, LANES), F32)], axis=0
        )

    tall = -(-2 * groups // ROWS) * ROWS
    real, imag = inverse_tiles(halo_rows, tall, back, twist)
    for a in range(radix):
        for g in range(groups):
            c, s, _ = correction(beside[a], angulars[g // 2], 2.0 * (g % 2) - 1.0)
            pair = slice(2 * g, 2 * g + 2)
            edge[0, a, pair, :] = real[a][pair] * c - imag[a][pair] * s
            edge[1, a, pair, :] = real[a][pair] * s + imag[a][pair] * c
    leaving = []
    for number in range(groups // 2):
        for a in range(radix):
            turns[0, a], turns[1, a], turns[2, a] = correction(speed[:, lanes(a)], angulars[number], 1.0)
        for which, out, home in ((0, source, source_out), (1, receiver, receiver_out)):
            sign = 2.0 * which - 1.0
            g = 2 * number + which
            real, imag = inverse_tiles(
                lambda k, part: data[g, k // half, (2 * (k % half) + part) * rows : (2 * (k % half) + part + 1) * rows, :],
                rows,
                back,
                twist,
            )
            for a in range(radix):
                c, s = turns[0, a], turns[1, a] * sign
                field[0, a] = real[a] * c - imag[a] * s
                field[1, a] = real[a] * s + imag[a] * c

            def store(part, a, value):
                out[part, number, :, lanes(a)] = value

            stencil(
                lambda part, a: field[part, a],
                lambda part, side, a: edge[part, a, 2 * g + side : 2 * g + side + 1, :],
                (radix, lambda a: turns[2, a]),
                sign,
                store,
            )
            leaving += copies((out.at[:, number], home.at[:, number]))
    for a in range(radix):
        total = jnp.zeros((rows, LANES), F32)
        for number in range(groups // 2):
            for part in (0, 1):
                total = total + source[part, number, :, lanes(a)] * receiver[part, number, :, lanes(a)]
        image[:, lanes(a)] = total
    done(leaving)


def last(ids, angulars, speed, beside, pieces, tab, groups):
    rows, width = speed.shape
    radix = width // LANES
    out = jax.ShapeDtypeStruct((2, groups // 2, rows, width), F32)
    return call(
        functools.partial(last_kernel, groups, rows),
        "last",
        (out, out, jax.ShapeDtypeStruct((rows, width), F32)),
        [SMEM] * 2 + [VMEM] * 4 + [ANY] * (2 * groups),
        (ANY, ANY, VMEM),
        [
            pltpu.VMEM(out.shape, F32),
            pltpu.VMEM(out.shape, F32),
            pltpu.VMEM((groups, 2, radix * rows + 2 * radix, LANES), F32),
            pltpu.VMEM((2, radix, rows, LANES), F32),
            pltpu.VMEM((2, radix, 2 * groups, LANES), F32),
            pltpu.VMEM((3, radix, rows, LANES), F32),
            pltpu.SemaphoreType.DMA((3 * groups,)),
        ],
        12,
        8000000000,
        8000000,
        (ids, angulars, tab["right_inverse"], tab["twist_y"], speed, beside, *pieces),
    )


def gather_order(groups):
    order = [0]
    for bit in bits(groups):
        order += [e ^ bit for e in order]
    return order


def after(value, *others):
    return lax.optimization_barrier((value, others))[0]


def bits(count):
    return [1 << n for n in reversed(range(count.bit_length() - 1))]


def centered(position, length):
    shifted = jnp.where(position < length // 2, position, position - length)
    return shifted.astype(F32) * (2.0 * math.pi / length)


def column_filter(angular, sign, height, width, first_block, blocks):
    radix_x, radix_y = height // LANES, width // LANES
    inner = jnp.arange(LANES, dtype=jnp.int32)
    wave_x = centered(jnp.arange(radix_x, dtype=jnp.int32)[:, None] + radix_x * inner[None, :], height)
    wave_y = centered(first_block + jnp.arange(blocks, dtype=jnp.int32)[:, None] + radix_y * inner[None, :], width)
    wave_x = wave_x[None, :, :, None]
    wave_y = wave_y[:, None, None, :]
    argument = angular * angular - (wave_x * wave_x + wave_y * wave_y)
    radius = step_length * jnp.sqrt(jnp.abs(argument))
    travel = argument >= 0.0
    scale = 1.0 / (height * width)
    cosine, ratio = turn(jnp.where(travel, radius * radius, 0.0))
    real = jnp.where(travel, cosine, jnp.exp(-radius)) * scale
    imag = jnp.where(travel, ratio * radius, 0.0) * (sign * scale)
    return real, imag


def local(source_field, receiver_field, velocity, slice_owner):
    freq_local, rows, width = source_field.shape[1:]
    strips = lax.axis_size("strip")
    planes = lax.axis_size("freq")
    height = rows * strips
    groups = 2 * freq_local
    members = strips // groups
    across = members // 2
    radix = width // LANES
    half = radix // 2
    freq_total = freq_local * planes
    me = lax.axis_index("strip")
    plane = lax.axis_index("freq")
    z, y, core = me // members, (me // 2) % across, me % 2
    ids = jnp.stack([z, y, core, plane]).astype(jnp.int32)

    def swap(value, bit):
        return lax.ppermute(value, "strip", [(i, i ^ bit) for i in range(strips)])

    def swap_z(value, e):
        return swap(value, e * members)

    def swap_y(value, r):
        return swap(value, 2 * r)

    def swap_core(value):
        return swap(value, 1)

    def ahead_plane(value, k):
        return lax.ppermute(value, "freq", [(i, (i + k) % planes) for i in range(planes)])

    forward, inverse = point_tables()
    stack = lambda table: jnp.asarray(np.stack(halves(table)))
    both = lambda table: jnp.asarray(np.concatenate(halves(table)))
    tab = {
        "right_forward": stack(forward),
        "right_inverse": stack(inverse),
        "left_forward": both(forward.T),
        "left_inverse": both(inverse.T),
        "twist_y": jnp.asarray(twiddles(radix)[:, :, None, :]),
        "twist_x": jnp.asarray(np.repeat(twiddles(height // LANES)[..., None], LANES, axis=-1)),
    }

    slots = velocity.shape[0]
    shelf = jnp.stack([velocity] + [ahead_plane(velocity, k) for k in range(1, planes)])

    def own_slice(depth):
        number = slice_owner[depth]
        return lax.dynamic_slice(
            shelf,
            ((plane - number // slots) % planes, number % slots, 0, 0),
            (1, 1, rows, width),
        )[0, 0]

    speeds = [own_slice(depth) for depth in range(DEPTHS)]

    final, top = groups - 1, groups // 2
    messages = {}
    order = [top, 0] + [e for e in range(1, final) if e != top] + [final]
    made = list(first_transform(ids, source_field, receiver_field, order, final, tab))
    for e in order:
        messages[e] = [made.pop(0) for _ in range(half // 2 if e == final else 1)]
    pieces, full = {0: messages[0]}, {}

    def share(e, *waits):
        ready = [after(piece, wait) for piece, wait in zip(pieces[e], waits)] if waits else pieces[e]
        mine = [pieces[e]] + [[] for r in range(1, across)]
        for piece in ready:
            sent = [swap_y(after(piece, mine[r][-1:]), r) for r in range(1, across)]
            for r in range(1, across):
                mine[r].append(sent[r - 1])
        full[e] = [lot for own in mine for lot in (own, [swap_core(piece) for piece in own])]

    angular = omega_top * (plane * freq_local + z // 2 + 1).astype(F32) / freq_total
    sign = jnp.where(z % 2 == 0, -1.0, 1.0).astype(F32)
    filt = column_filter(angular, sign, height, width, core * half, half)
    share(0, shelf)
    for e in range(final - 1, 0, -1):
        pieces[e] = [swap_z(messages[e][0], e)]
    for e in range(1, final):
        share(e)
    book = jnp.concatenate([speeds[0], speeds[1][:1], speeds[1][-1:], jnp.zeros((6, width), F32)])
    book = jnp.swapaxes(book.reshape(rows + 8, -1, LANES), 0, 1)[None]
    books = [(book, [0]), (swap_z(book, top), [top])]
    pieces[final] = []
    for i, message in enumerate(messages[final]):
        ready = (pieces[1], full[0][2]) if i == 0 else (pieces[top], full[1][2], filt)
        pieces[final].append(swap_z(after(message, ready), final))
    for bit in bits(groups)[1:]:
        book, offsets = jnp.concatenate([held for held, _ in books]), [e for _, lot in books for e in lot]
        books = [(book, offsets), (swap_z(book, bit), [e ^ bit for e in offsets])]
    share(final, *([(full[0], full[1][2])] + [(full[1], full[top][2])] * (half // 2 - 1)))
    books = [(held, lot, 0) for held, lot in books] + [
        (swap_y(held if n == 0 else after(held, pieces[final]), r), lot, r)
        for n, (held, lot) in enumerate(books)
        for r in range(1, across)
    ]
    edges = lambda held: jnp.concatenate([held[:, :, :8], held[:, :, rows - 8 :]], axis=2)
    facing = [swap_core(edges(held)) for held, _, _ in books]
    scales = jnp.stack([angular, sign])
    chosen = [piece for e in range(groups) for lot in full[e] for piece in lot]
    mine, give = enter_columns(ids, chosen, filt, tab, groups, across, rows, half)
    other = swap_core(give)
    *factors, beside = prepare(ids, scales, books, facing, groups, across, rows)
    mine, give, near, far = middle(ids, mine, other, factors, tab, groups, across, rows, half)

    other = swap_core(give)
    outs = leave_columns(ids, mine, other, filt, tab, groups, across, rows, half)

    arrived = []
    for e in range(groups):
        piece = swap_z(outs[e], e) if e else outs[e]
        arrived += [piece, swap_core(piece)]

    facing = swap_z(far, 1)
    facing = after(facing, arrived[2])
    image = near[0] * facing[0] + near[1] * facing[1]

    wide = width // planes

    def spread(value):
        part = lambda k: lax.dynamic_slice_in_dim(value, ((plane + k) % planes) * wide, wide, axis=value.ndim - 1)
        total = part(0)
        for k in range(1, planes):
            total = total + ahead_plane(part(k), k)
        return total

    image = spread(image)
    first_image = lax.dynamic_index_in_dim(image, z // 2, 0, keepdims=False)
    for d in range(1, groups // 2):
        piece = lax.dynamic_index_in_dim(image, (z // 2) ^ d, 0, keepdims=False)
        first_image = first_image + swap_z(piece, 2 * d)

    numbers = jnp.arange(freq_local, dtype=jnp.int32) + plane * freq_local
    angulars = omega_top * (numbers + 1).astype(F32) / freq_total
    source_out, receiver_out, last_image = last(ids, angulars, speeds[1], beside, arrived, tab, groups)
    depth_image = jnp.stack([first_image, spread(last_image)])
    return (depth_image, source_out, receiver_out)


def solution(mesh):
    return jax.shard_map(
        local,
        mesh=mesh,
        in_specs=(
            P(None, "freq", "strip", None),
            P(None, "freq", "strip", None),
            P("freq", "strip", None),
            P(),
        ),
        out_specs=(
            P(None, "strip", "freq"),
            P(None, "freq", "strip", None),
            P(None, "freq", "strip", None),
        ),
        check_vma=False,
    )
```
